32 devices in a mesh: seq: 8 (over z, y), head: 4 (over x, core).
Axes of the slice: x: 2, y: 2, z: 4, core: 2. Of those that a mesh axis runs over, the one named last changes fastest.
Arguments:
- queries: bfloat16 [2048, 4096], P(('seq', 'head')), may hold values from -1 to 1
- keys: bfloat16 [2048, 1024], P(('seq', 'head')), may hold values from -2.5 to 2.5
- values: bfloat16 [2048, 1024], P(('seq', 'head')), may hold values from -3 to 3
- outputs_saved: bfloat16 [2048, 4096], P(('seq', 'head')), may hold values from -3 to 3
- grad_out: bfloat16 [2048, 4096], P(('seq', 'head')), may hold values from -3 to 3
- lse: float32 [2048, 32], P('seq', 'head'), may hold values from 2.5 to 4
- block_lists: int32 [16, 32, 4], P(None, 'head'), may hold values from 0 to 31, as said below
Outputs:
- grad_queries: bfloat16 [2048, 4096], P(('seq', 'head'))
- grad_keys: bfloat16 [2048, 1024], P(('seq', 'head'))
- grad_values: bfloat16 [2048, 1024], P(('seq', 'head'))
The draws below stay inside these ranges and needn't reach their ends.
Inputs may be any that keep to these rules, and one draw needn't show every extreme that they name: `block_lists`: key block j lies in sequence shard j // 4. No query block lists a key block of its own sequence shard. For the query blocks of one sequence shard and the 8 query heads held by one device along `head`, at most 10 listed block lies in any one other sequence shard; a few shards are listed far more often than the others.
All inputs are finite; a program needn't handle non-finite values.
Results may differ from the reference program's by a relative error of at most 0.011.
Values may be sent and summed in bfloat16 or wider, within the bound.
No kernel may reach another device: no remote copies, remote signals or barrier semaphores. Data moves between devices by JAX's collectives and lax.ppermute only.
A program may use at most 128 MiB of HBM per device.

```python
import jax
import jax.numpy as jnp
from jax import lax

QH = 32
KVH = 8
HD = 128
QB = 128
KB = 64
NSEL = 4
TOKENS = 2048
NQB = 16
NKB = 32
NQB_DEV = 2
NKB_DEV = 4
GROUP = 4
N_SEQ = 8
N_HEAD = 4


def draw_block_lists(key, part):
    key = jax.random.fold_in(key, 11)
    neighbour_count = N_SEQ
    heads_dev = QH // N_HEAD
    request_count = NQB_DEV * heads_dev * NSEL
    favoured_count = max(1, neighbour_count // 16)
    key_fav, key_noise, key_shuffle, key_local = jax.random.split(key, 4)
    preferred_blocks = jax.random.permutation(key_fav, neighbour_count - 2)[:favoured_count] + 1
    extra_reward = jnp.zeros((neighbour_count,), jnp.int32).at[preferred_blocks].set(1)
    extra_reward = extra_reward.at[neighbour_count - 1].set(3).at[0].set(2)
    random_jitter = jax.random.randint(key_noise, (neighbour_count, N_HEAD, neighbour_count), 0, 1 << 16)
    owning_devices = jnp.arange(neighbour_count, dtype=jnp.int32)
    logit_scores = (extra_reward[None, None, :] * (1 << 16) + random_jitter) * neighbour_count + owning_devices[None, None, :]
    own_self = owning_devices[:, None, None] == owning_devices[None, None, :]
    logit_scores = jnp.where(own_self, -1, logit_scores)
    ranked = jnp.argsort(-logit_scores, axis=-1, stable=True).astype(jnp.int32)
    shuffle_keys = jax.random.randint(key_shuffle, (neighbour_count, N_HEAD, request_count), 0, 1 << 20)
    shuffle_keys = shuffle_keys * request_count + jnp.arange(request_count, dtype=jnp.int32)[None, None, :]
    shuffled = jnp.argsort(shuffle_keys, axis=-1, stable=True).astype(jnp.int32)
    rank_pos = shuffled % (neighbour_count - 1)
    owner_of = jnp.take_along_axis(ranked, rank_pos, axis=-1)
    local_block = jax.random.randint(key_local, (neighbour_count, N_HEAD, request_count), 0, NKB_DEV)
    local_block = jnp.where(rank_pos == 0, NKB_DEV - 1, jnp.where(rank_pos == 1, 0, local_block))
    chosen = owner_of * NKB_DEV + local_block
    chosen = chosen.reshape(neighbour_count, N_HEAD, NQB_DEV, heads_dev, NSEL).transpose(0, 2, 1, 3, 4)
    return chosen.reshape(NQB, QH, NSEL).astype(jnp.int32)


def steps_of(own_key, extent, pieces, least, top_value):
    def one(position, blocks):
        steps = jax.random.uniform(jax.random.fold_in(jax.random.fold_in(own_key, 6), position), (blocks,), jnp.float32, least / len(pieces), top_value / len(pieces))
        return jnp.repeat(jnp.exp(steps), extent[position] // blocks).reshape((-1,) + (1,) * (len(extent) - position - 1))

    level = one(*pieces[0])
    for cut in pieces[1:]:
        level = level * one(*cut)
    return level


def normal_values(key, dims, spread, reach, cuts=(), kind=jnp.bfloat16):
    entries = spread * jax.random.normal(key, dims, jnp.float32)
    if cuts:
        entries = entries * steps_of(key, dims, cuts, -0.22, 0.18)
    return jnp.clip(entries, -reach, reach).astype(kind)


def setup_inputs(seed: int = 0) -> dict:
    arg_keys = jax.random.split(jax.random.key(seed), 8)
    return {
        "queries": normal_values(arg_keys[0], (TOKENS, QH * HD), 0.4, 1.0, ((0, 32),)),
        "keys": normal_values(arg_keys[1], (TOKENS, KVH * HD), 1.0, 2.5, ((0, 32),)),
        "values": normal_values(arg_keys[2], (TOKENS, KVH * HD), 1.0, 3.0, ((0, 32),)),
        "outputs_saved": normal_values(arg_keys[3], (TOKENS, QH * HD), 1.0, 3.0, ((0, 32),)),
        "grad_out": normal_values(arg_keys[4], (TOKENS, QH * HD), 1.0, 3.0, ((0, 32),)),
        "lse": jnp.clip(2.5 + 1.5 * jax.random.uniform(arg_keys[5], (TOKENS, QH), jnp.float32) ** steps_of(arg_keys[5], (TOKENS, QH), ((0, 8), (1, 4)), -0.2, 0.2), 2.5, 4.0),
        "block_lists": draw_block_lists(jax.random.fold_in(arg_keys[7], 71), 0),
    }


def rounded(tensor):
    return lax.optimization_barrier(tensor.astype(jnp.bfloat16)).astype(jnp.float32)


def remote_terms(q_rows, o_grad, lse_rows, delta_rows, k_rows, v_rows):
    scaling = HD ** -0.5
    q_full = q_rows.astype(jnp.float32)
    o_full = o_grad.astype(jnp.float32)
    k_full = k_rows.astype(jnp.float32)
    v_full = v_rows.astype(jnp.float32)
    logit_scores = jnp.einsum("nkd,nqd->nkq", k_full, q_full) * scaling
    probability = jnp.exp(logit_scores - lse_rows[:, None, :])
    grad_prob = jnp.einsum("nkd,nqd->nkq", v_full, o_full)
    score_gradient = probability * (grad_prob - delta_rows[:, None, :])
    prob_low = rounded(probability)
    score_low = rounded(score_gradient)
    dq_part = (jnp.einsum("nkq,nkd->nqd", score_low, k_full) * scaling).astype(jnp.bfloat16)
    dk_part = (jnp.einsum("nkq,nqd->nkd", score_low, q_full) * scaling).astype(jnp.bfloat16)
    dv_part = jnp.einsum("nkq,nqd->nkd", prob_low, o_full).astype(jnp.bfloat16)
    return dq_part, dk_part, dv_part


def reference(queries, keys, values, outputs_saved, grad_out, lse, block_lists):
    scaling = HD ** -0.5
    ratio = QB // KB
    key_blocks = keys.reshape(NKB, KB, KVH, HD)
    value_blocks = values.reshape(NKB, KB, KVH, HD)
    kv_of_head = jnp.broadcast_to((jnp.arange(QH, dtype=jnp.int32) // GROUP)[:, None], (QH, NSEL)).reshape(-1)
    causal = lax.broadcasted_iota(jnp.int32, (QB, QB), 0) <= lax.broadcasted_iota(jnp.int32, (QB, QB), 1)

    def per_block(totals, block_index):
        grad_k, grad_v = totals
        row_start = block_index * QB
        q_rows = lax.dynamic_slice_in_dim(queries, row_start, QB, 0).reshape(QB, QH, HD)
        do_rows = lax.dynamic_slice_in_dim(grad_out, row_start, QB, 0).reshape(QB, QH, HD)
        o_rows = lax.dynamic_slice_in_dim(outputs_saved, row_start, QB, 0).reshape(QB, QH, HD)
        lse_rows = lax.dynamic_slice_in_dim(lse, row_start, QB, 0)
        delta_rows = jnp.sum(do_rows.astype(jnp.float32) * o_rows.astype(jnp.float32), axis=-1)
        k_rows = lax.dynamic_slice_in_dim(keys, row_start, QB, 0).reshape(QB, KVH, HD).astype(jnp.float32)
        v_rows = lax.dynamic_slice_in_dim(values, row_start, QB, 0).reshape(QB, KVH, HD).astype(jnp.float32)
        q_five = q_rows.reshape(QB, KVH, GROUP, HD).astype(jnp.float32)
        do_five = do_rows.reshape(QB, KVH, GROUP, HD).astype(jnp.float32)
        lse_t = lse_rows.reshape(QB, KVH, GROUP).transpose(1, 2, 0)
        delta_t = delta_rows.reshape(QB, KVH, GROUP).transpose(1, 2, 0)
        logit_scores = jnp.einsum("shd,qhgd->hgsq", k_rows, q_five) * scaling
        probability = jnp.where(causal, jnp.exp(logit_scores - lse_t[:, :, None, :]), jnp.float32(0.0))
        grad_prob = jnp.einsum("shd,qhgd->hgsq", v_rows, do_five)
        score_gradient = probability * (grad_prob - delta_t[:, :, None, :])
        prob_low = rounded(probability)
        score_low = rounded(score_gradient)
        dq_own = (jnp.einsum("hgsq,shd->qhgd", score_low, k_rows) * scaling).reshape(QB, QH, HD)
        dk_own = jnp.einsum("hgsq,qhgd->shd", score_low, q_five) * scaling
        dv_own = jnp.einsum("hgsq,qhgd->shd", prob_low, do_five)
        chosen = block_lists[block_index].reshape(-1)
        k_sel = key_blocks[chosen, :, kv_of_head]
        v_sel = value_blocks[chosen, :, kv_of_head]
        q_sel = jnp.repeat(q_rows.transpose(1, 0, 2), NSEL, axis=0)
        do_sel = jnp.repeat(do_rows.transpose(1, 0, 2), NSEL, axis=0)
        lse_sel = jnp.repeat(lse_rows.T, NSEL, axis=0)
        delta_sel = jnp.repeat(delta_rows.T, NSEL, axis=0)
        dq_part, dk_part, dv_part = remote_terms(q_sel, do_sel, lse_sel, delta_sel, k_sel, v_sel)
        dq_listed = dq_part.astype(jnp.float32).reshape(QH, NSEL, QB, HD).sum(axis=1).transpose(1, 0, 2)
        dq_rows = (dq_own + dq_listed).astype(jnp.bfloat16).reshape(QB, QH * HD)
        block_start = (block_index * ratio).astype(jnp.int32)
        zero = jnp.int32(0)
        old_k = lax.dynamic_slice(grad_k, (block_start, zero, zero, zero), (ratio, KB, KVH, HD))
        old_v = lax.dynamic_slice(grad_v, (block_start, zero, zero, zero), (ratio, KB, KVH, HD))
        grad_k = lax.dynamic_update_slice(grad_k, old_k + dk_own.reshape(ratio, KB, KVH, HD), (block_start, zero, zero, zero))
        grad_v = lax.dynamic_update_slice(grad_v, old_v + dv_own.reshape(ratio, KB, KVH, HD), (block_start, zero, zero, zero))
        grad_k = grad_k.at[chosen, :, kv_of_head].add(dk_part.astype(jnp.float32))
        grad_v = grad_v.at[chosen, :, kv_of_head].add(dv_part.astype(jnp.float32))
        return (grad_k, grad_v), dq_rows

    start_totals = (jnp.zeros((NKB, KB, KVH, HD), jnp.float32), jnp.zeros((NKB, KB, KVH, HD), jnp.float32))
    (grad_k, grad_v), dq_blocks = lax.scan(per_block, start_totals, jnp.arange(NQB, dtype=jnp.int32))
    grad_queries = dq_blocks.reshape(TOKENS, QH * HD)
    grad_keys = grad_k.reshape(TOKENS, KVH * HD).astype(jnp.bfloat16)
    grad_values = grad_v.reshape(TOKENS, KVH * HD).astype(jnp.bfloat16)
    return (grad_queries, grad_keys, grad_values)
```

```python
import functools

import jax
import jax.numpy as jnp
from jax import lax
from jax.experimental import pallas as pl
from jax.experimental.pallas import tpu as pltpu
from jax.sharding import PartitionSpec as P

HD = 128
QB = 128
KB = 64
NSEL = 4
GROUP = 4
SCALE = HD ** (-0.5)
STAT = 16

VMEM = pl.BlockSpec(memory_space=pltpu.VMEM)
SMEM = pl.BlockSpec(memory_space=pltpu.SMEM)
NT = (((1,), (1,)), ((), ()))
TN = (((0,), (0,)), ((), ()))
PARAMS = pltpu.CompilerParams(vmem_limit_bytes=48 * 1024 * 1024)


def dot(a, b, dims=(((1,), (0,)), ((), ()))):
    return lax.dot_general(a, b, dims, preferred_element_type=jnp.float32)


def pack_kv_kernel(k_ref, v_ref, out_ref):
    for g in range(out_ref.shape[0]):
        cols = slice(g * HD, (g + 1) * HD)
        out_ref[g, :, :HD] = k_ref[:, cols]
        out_ref[g, :, HD:] = v_ref[:, cols]


def pack_kv(keys, values):
    tokens, width = keys.shape
    return pl.pallas_call(
        pack_kv_kernel,
        out_shape=jax.ShapeDtypeStruct((width // HD, tokens, 2 * HD), jnp.bfloat16),
        in_specs=[VMEM, VMEM],
        out_specs=VMEM,
        compiler_params=PARAMS,
    )(keys, values)


def three_pieces(x):
    hi = x.astype(jnp.bfloat16)
    rest = x - hi.astype(jnp.float32)
    mid = rest.astype(jnp.bfloat16)
    low = (rest - mid.astype(jnp.float32)).astype(jnp.bfloat16)
    return hi, mid, low


def pack_q_kernel(q_ref, do_ref, o_ref, out_ref):
    peers, rows, _ = out_ref.shape
    heads = (rows - STAT) // KB
    lane = lax.broadcasted_iota(jnp.int32, (KB, HD), 1)
    delta = jnp.zeros((KB, HD), jnp.float32)
    for t in range(peers):
        for h in range(heads):
            head = t * heads + h
            cols = slice(head * HD, (head + 1) * HD)
            do = do_ref[:, cols]
            out_ref[t, h * KB : (h + 1) * KB, :HD] = q_ref[:, cols]
            out_ref[t, h * KB : (h + 1) * KB, HD:] = do
            products = do.astype(jnp.float32) * o_ref[:, cols].astype(jnp.float32)
            total = jnp.sum(products, axis=-1, keepdims=True)
            delta = jnp.where(lane == head, total, delta)
    by_head = delta.T
    for t in range(peers):
        hi, mid, low = three_pieces(by_head[t * heads : (t + 1) * heads])
        base = heads * KB
        zero = jnp.zeros((heads, HD - KB), jnp.bfloat16)
        first = jnp.concatenate([hi, zero, mid, zero], axis=1)
        second = jnp.concatenate([low, zero, zero, jnp.zeros_like(low)], axis=1)
        out_ref[t, base : base + STAT, :] = jnp.concatenate([first, second], axis=0)


def pack_q(queries, grad_out, outputs_saved, peers):
    tokens, width = queries.shape
    heads = width // HD // peers
    return pl.pallas_call(
        pack_q_kernel,
        out_shape=jax.ShapeDtypeStruct((peers, heads * tokens + STAT, 2 * HD), jnp.bfloat16),
        in_specs=[VMEM] * 3,
        out_specs=VMEM,
        compiler_params=PARAMS,
    )(queries, grad_out, outputs_saved)


def attend_kernel(
    slot_ref, kv_ref, own_kv_ref, qdo_ref, lse_ref, dq_ref, part_ref, own_ref, sums, stats
):
    peers, rows, _ = qdo_ref.shape
    heads = (rows - STAT) // KB
    kv_heads = heads // GROUP
    blocks = peers * KB // QB
    base = heads * KB
    sums[...] = jnp.zeros_like(sums)
    own_ref[...] = jnp.zeros_like(own_ref)
    lse = lse_ref[...].T
    pieces = []
    for t in range(peers):
        first = qdo_ref[t, base : base + heads, :].astype(jnp.float32)
        second = qdo_ref[t, base + heads : base + 2 * heads, :].astype(jnp.float32)
        pieces.append(first[:, :KB] + first[:, HD : HD + KB] + second[:, :KB])
    delta = jnp.concatenate(pieces, axis=1)
    stats[0] = lse
    stats[1] = delta
    key_row = lax.broadcasted_iota(jnp.int32, (QB, QB), 0)
    query_row = lax.broadcasted_iota(jnp.int32, (QB, QB), 1)
    causal = key_row <= query_row
    for b in range(blocks):
        for h in range(heads):
            g = h // GROUP
            rows_h = slice(h * KB, (h + 1) * KB)
            q = jnp.concatenate([qdo_ref[2 * b + i, rows_h, :HD] for i in range(2)], axis=0)
            do = jnp.concatenate([qdo_ref[2 * b + i, rows_h, HD:] for i in range(2)], axis=0)
            slots = [slot_ref[(b * heads + h) * NSEL + n] for n in range(NSEL)]
            own = [(2 * b + i) * kv_heads + g for i in range(2)]
            listed = [kv_ref[s] for s in slots] + [own_kv_ref[u] for u in own]
            kv = jnp.concatenate(listed, axis=0)
            k = kv[:, :HD]
            v = kv[:, HD:]
            lse_row = stats[0, h : h + 1, b * QB : (b + 1) * QB]
            delta_row = stats[1, h : h + 1, b * QB : (b + 1) * QB]
            prob = jnp.exp(dot(k, q, NT) * SCALE - lse_row)
            own_prob = jnp.where(causal, prob[NSEL * KB :], 0.0)
            prob = jnp.concatenate([prob[: NSEL * KB], own_prob], axis=0)
            score = (prob * (dot(v, do, NT) - delta_row)).astype(jnp.bfloat16)
            prob = prob.astype(jnp.bfloat16)
            dq = dot(score, k, TN) * SCALE
            for i in range(2):
                dq_ref[2 * b + i, :, h * HD : (h + 1) * HD] = dq[i * KB : (i + 1) * KB].astype(
                    jnp.bfloat16
                )
            dk = dot(score, q) * SCALE
            dv = dot(prob, do)
            for n in range(NSEL):
                part = slice(n * KB, (n + 1) * KB)
                sums[slots[n], :, :HD] += dk[part]
                sums[slots[n], :, HD:] += dv[part]
            for i in range(2):
                part = slice((NSEL + i) * KB, (NSEL + i + 1) * KB)
                own_ref[own[i], :, :HD] += dk[part]
                own_ref[own[i], :, HD:] += dv[part]
    part_ref[...] = sums[...].astype(jnp.bfloat16)


def attend(slots, kv_slots, own_kv, qdo, lse):
    peers, rows, _ = qdo.shape
    heads = (rows - STAT) // KB
    return pl.pallas_call(
        attend_kernel,
        out_shape=(
            jax.ShapeDtypeStruct((peers, KB, heads * HD), jnp.bfloat16),
            jax.ShapeDtypeStruct(kv_slots.shape, jnp.bfloat16),
            jax.ShapeDtypeStruct(own_kv.shape, jnp.float32),
        ),
        in_specs=[SMEM, VMEM, VMEM, VMEM, VMEM],
        out_specs=(VMEM, VMEM, VMEM),
        scratch_shapes=[
            pltpu.VMEM(kv_slots.shape, jnp.float32),
            pltpu.VMEM((2, heads, peers * KB), jnp.float32),
        ],
        compiler_params=PARAMS,
    )(slots, kv_slots, own_kv, qdo, lse)


def unpack_kernel(dq_ref, dkv_ref, gq_ref, gk_ref, gv_ref):
    peers, _, width = dq_ref.shape
    for t in range(peers):
        gq_ref[:, t * width : (t + 1) * width] = dq_ref[t]
    for g in range(dkv_ref.shape[0]):
        gk_ref[:, g * HD : (g + 1) * HD] = dkv_ref[g, :, :HD]
        gv_ref[:, g * HD : (g + 1) * HD] = dkv_ref[g, :, HD:]


def unpack(dq, dkv):
    peers, tokens, width = dq.shape
    kv_heads = dkv.shape[0]
    return pl.pallas_call(
        unpack_kernel,
        out_shape=(
            jax.ShapeDtypeStruct((tokens, peers * width), jnp.bfloat16),
            jax.ShapeDtypeStruct((tokens, kv_heads * HD), jnp.bfloat16),
            jax.ShapeDtypeStruct((tokens, kv_heads * HD), jnp.bfloat16),
        ),
        in_specs=[VMEM, VMEM],
        out_specs=(VMEM, VMEM, VMEM),
        compiler_params=PARAMS,
    )(dq, dkv)


def body(queries, keys, values, outputs_saved, grad_out, lse, block_lists):
    peers = lax.axis_size("head")
    shards = lax.axis_size("seq")
    me = lax.axis_index("seq")
    heads = lse.shape[1]
    kv_heads = heads // GROUP
    key_count = peers
    units = key_count * kv_heads

    own_kv = lax.all_to_all(pack_kv(keys, values), "head", 0, 0, tiled=True)

    per_peer = block_lists.reshape(shards, -1)
    requests = per_peer.shape[1]
    order = jnp.arange(requests, dtype=jnp.int32)
    group_of = order % (heads * NSEL) // (NSEL * GROUP)
    capacity = -(-requests // (shards - 1))
    dense = units <= capacity

    if dense:
        kv_slots = lax.all_gather(own_kv, "seq", axis=0, tiled=True)
        mine = lax.dynamic_index_in_dim(per_peer, me, 0, keepdims=False)
        slots = mine * kv_heads + group_of
    else:
        owner = per_peer // key_count
        earlier = (owner[:, :, None] == owner[:, None, :]) & (order[None, :] < order[:, None])
        position = jnp.sum(earlier.astype(jnp.int32), axis=2)
        slots = lax.dynamic_index_in_dim(owner * capacity + position, me, 0, keepdims=False)
        hits = (owner == me)[:, :, None] & (position[:, :, None] == jnp.arange(capacity))
        hits = hits.astype(jnp.int32)
        used = jnp.sum(hits, axis=1).reshape(-1)
        wanted = (per_peer % key_count) * kv_heads + group_of[None, :]
        wanted = jnp.sum(hits * wanted[:, :, None], axis=1).reshape(-1)
        kv_slots = lax.all_to_all(own_kv[wanted], "seq", 0, 0, tiled=True)

    packed = pack_q(queries, grad_out, outputs_saved, peers)
    qdo = lax.all_to_all(packed, "head", 0, 0, tiled=True)
    dq, parts, own = attend(slots, kv_slots, own_kv, qdo, lse)
    dq = lax.all_to_all(dq, "head", 0, 0, tiled=True)

    if dense:
        total = lax.psum_scatter(parts, "seq", scatter_dimension=0, tiled=True)
        total = total.astype(jnp.float32) + own
    else:
        parts = lax.all_to_all(parts, "seq", 0, 0, tiled=True)
        chosen = (jnp.arange(units)[:, None] == wanted[None, :]) & (used[None, :] > 0)
        total = jnp.dot(
            chosen.astype(jnp.bfloat16),
            parts.reshape(parts.shape[0], -1),
            preferred_element_type=jnp.float32,
        )
        total = total.reshape(own.shape) + own
    dkv = lax.all_to_all(total.astype(jnp.bfloat16), "head", 0, 0, tiled=True)
    return unpack(dq, dkv)


def solution(mesh):
    rows = P(("seq", "head"), None)
    in_specs = (rows, rows, rows, rows, rows, P("seq", "head"), P(None, "head", None))
    return jax.shard_map(
        body, mesh=mesh, in_specs=in_specs, out_specs=(rows, rows, rows), check_vma=False
    )
```

```python
import functools

import jax
import jax.numpy as jnp
from jax import lax
from jax.experimental import pallas as pl
from jax.experimental.pallas import tpu as pltpu
from jax.sharding import PartitionSpec as P

HD = 128
QB = 128
KB = 64
NSEL = 4
GROUP = 4
SCALE = HD ** (-0.5)
STAT = 16

VMEM = pl.BlockSpec(memory_space=pltpu.VMEM)
ANY = pl.BlockSpec(memory_space=pl.ANY)
HBM = pl.BlockSpec(memory_space=pltpu.HBM)
SMEM = pl.BlockSpec(memory_space=pltpu.SMEM)
NT = (((1,), (1,)), ((), ()))
TN = (((0,), (0,)), ((), ()))
PARAMS = pltpu.CompilerParams(vmem_limit_bytes=24 * 1024 * 1024)


def dot(a, b, dims=(((1,), (0,)), ((), ()))):
    return lax.dot_general(a, b, dims, preferred_element_type=jnp.float32)


def lanes(index, width):
    return pl.ds(pl.multiple_of(index * width, width), width)


def run_copies(pairs, sems):
    copies = [
        pltpu.make_async_copy(source, target, sems.at[i])
        for i, (source, target) in enumerate(pairs)
    ]
    for copy in copies:
        copy.start()
    return copies


def pack_kv_kernel(peers, me_ref, k_ref, v_ref, *refs):
    out_refs, sems = refs[:peers], refs[peers]
    kv_heads = out_refs[0].shape[0]
    pairs = []
    for c, out_ref in reversed(list(enumerate(out_refs))):
        for g in range(kv_heads):
            cols = lanes((me_ref[0] ^ c) * kv_heads + g, HD)
            pairs.append((k_ref.at[:, cols], out_ref.at[g, :, pl.ds(0, HD)]))
            pairs.append((v_ref.at[:, cols], out_ref.at[g, :, pl.ds(HD, HD)]))
    for copy in run_copies(pairs, sems):
        copy.wait()


def pack_kv(me, keys, values, peers):
    tokens, width = keys.shape
    kv_heads = width // HD // peers
    piece = jax.ShapeDtypeStruct((kv_heads, tokens, 2 * HD), jnp.bfloat16)
    return pl.pallas_call(
        functools.partial(pack_kv_kernel, peers),
        out_shape=(piece,) * peers,
        in_specs=[SMEM, HBM, HBM],
        out_specs=(VMEM,) * peers,
        scratch_shapes=[pltpu.SemaphoreType.DMA((2 * peers * kv_heads,))],
        compiler_params=PARAMS,
    )(me, keys, values)


def three_pieces(x):
    hi = x.astype(jnp.bfloat16)
    rest = x - hi.astype(jnp.float32)
    mid = rest.astype(jnp.bfloat16)
    low = (rest - mid.astype(jnp.float32)).astype(jnp.bfloat16)
    return hi, mid, low


def pack_q_kernel(peers, me_ref, q_any, do_any, o_any, *refs):
    out_refs = refs[:peers]
    q_ref, do_ref, o_ref, sems = refs[peers:]
    for copy in run_copies([(q_any, q_ref), (do_any, do_ref), (o_any, o_ref)], sems):
        copy.wait()
    heads = (out_refs[0].shape[0] - STAT) // KB
    lane = lax.broadcasted_iota(jnp.int32, (KB, HD), 1)
    delta = jnp.zeros((KB, HD), jnp.float32)
    for c, out_ref in enumerate(out_refs):
        for h in range(heads):
            cols = lanes((me_ref[0] ^ c) * heads + h, HD)
            do = do_ref[:, cols]
            out_ref[h * KB : (h + 1) * KB, :HD] = q_ref[:, cols]
            out_ref[h * KB : (h + 1) * KB, HD:] = do
            products = do.astype(jnp.float32) * o_ref[:, cols].astype(jnp.float32)
            total = jnp.sum(products, axis=-1, keepdims=True)
            delta = jnp.where(lane == c * heads + h, total, delta)
    by_head = delta.T
    for c, out_ref in enumerate(out_refs):
        hi, mid, low = three_pieces(by_head[c * heads : (c + 1) * heads])
        base = heads * KB
        zero = jnp.zeros((heads, HD - KB), jnp.bfloat16)
        first = jnp.concatenate([hi, zero, mid, zero], axis=1)
        second = jnp.concatenate([low, zero, zero, jnp.zeros_like(low)], axis=1)
        out_ref[base : base + STAT, :] = jnp.concatenate([first, second], axis=0)


def pack_q(me, queries, grad_out, outputs_saved, peers):
    tokens, width = queries.shape
    heads = width // HD // peers
    piece = jax.ShapeDtypeStruct((heads * tokens + STAT, 2 * HD), jnp.bfloat16)
    return pl.pallas_call(
        functools.partial(pack_q_kernel, peers),
        out_shape=(piece,) * peers,
        in_specs=[SMEM] + [HBM] * 3,
        out_specs=(VMEM,) * peers,
        scratch_shapes=[pltpu.VMEM(queries.shape, jnp.bfloat16)] * 3
        + [pltpu.SemaphoreType.DMA((3,))],
        compiler_params=PARAMS,
    )(me, queries, grad_out, outputs_saved)


def query_rows(qdo, c, h):
    rows = slice(h * KB, (h + 1) * KB)
    pair = (qdo[c], qdo[c ^ 1])
    q = jnp.concatenate([ref[rows, :HD] for ref in pair], axis=0)
    do = jnp.concatenate([ref[rows, HD:] for ref in pair], axis=0)
    return q, do


def own_kernel(peers, me_ref, own_kv_ref, stats_ref, *refs):
    qdo = refs[:peers]
    listed_refs = refs[peers : 2 * peers]
    dq_refs, own_ref = refs[2 * peers : 3 * peers], refs[3 * peers]
    heads = (qdo[0].shape[0] - STAT) // KB
    kv_heads = heads // GROUP
    key_row = lax.broadcasted_iota(jnp.int32, (QB, QB), 0)
    query_row = lax.broadcasted_iota(jnp.int32, (QB, QB), 1)
    swapped = jnp.where((me_ref[0] & 1) == 1, KB, 0)
    causal = (key_row ^ swapped) <= (query_row ^ swapped)
    for c in range(0, peers, 2):
        for g in range(kv_heads):
            own = [(c + i) * kv_heads + g for i in range(2)]
            kv = jnp.concatenate([own_kv_ref[u] for u in own], axis=0)
            k = kv[:, :HD]
            v = kv[:, HD:]
            dk = jnp.zeros((QB, HD), jnp.float32)
            dv = jnp.zeros((QB, HD), jnp.float32)
            for h in range(g * GROUP, (g + 1) * GROUP):
                q, do = query_rows(qdo, c, h)
                lse_row = stats_ref[0, h : h + 1, c * KB : c * KB + QB]
                delta_row = stats_ref[1, h : h + 1, c * KB : c * KB + QB]
                prob = jnp.where(causal, jnp.exp(dot(k, q, NT) * SCALE - lse_row), 0.0)
                score = (prob * (dot(v, do, NT) - delta_row)).astype(jnp.bfloat16)
                dq = dot(score, k, TN) * SCALE
                cols = slice(h * HD, (h + 1) * HD)
                for i in range(2):
                    part = listed_refs[c + i][:, cols] + dq[i * KB : (i + 1) * KB]
                    dq_refs[c + i][:, cols] = part.astype(jnp.bfloat16)
                dk += dot(score, q)
                dv += dot(prob.astype(jnp.bfloat16), do)
            for i in range(2):
                own_ref[own[i], :, :HD] = dk[i * KB : (i + 1) * KB] * SCALE
                own_ref[own[i], :, HD:] = dv[i * KB : (i + 1) * KB]


def own_terms(me, own_kv, stats, qdo, listed):
    peers = len(qdo)
    piece = jax.ShapeDtypeStruct(listed[0].shape, jnp.bfloat16)
    outs = pl.pallas_call(
        functools.partial(own_kernel, peers),
        out_shape=(piece,) * peers + (jax.ShapeDtypeStruct(own_kv.shape, jnp.float32),),
        in_specs=[SMEM] + [VMEM] * (2 + 2 * peers),
        out_specs=(VMEM,) * (peers + 1),
        compiler_params=PARAMS,
        cost_estimate=pl.CostEstimate(
            flops=335_000_000, bytes_accessed=4_000_000, transcendentals=260_000
        ),
    )(me, own_kv, stats, *qdo, *listed)
    return outs[:peers], outs[peers]


def row_stats(me, qdo, lse_ref, stats_ref):
    peers = len(qdo)
    heads = (qdo[0].shape[0] - STAT) // KB
    base = heads * KB
    lse_blocks = [lse_ref[:, c * KB : (c + 1) * KB] for c in range(peers)]
    for c in range(peers):
        first = qdo[c][base : base + heads, :].astype(jnp.float32)
        second = qdo[c][base + heads : base + 2 * heads, :].astype(jnp.float32)
        delta = first[:, :KB] + first[:, HD : HD + KB] + second[:, :KB]
        lse_here = lse_blocks[0]
        for t in range(1, peers):
            lse_here = jnp.where((me ^ c) == t, lse_blocks[t], lse_here)
        stats_ref[0, :, c * KB : (c + 1) * KB] = lse_here
        stats_ref[1, :, c * KB : (c + 1) * KB] = delta


def listed_kernel(peers, pieces, me_ref, slot_ref, lse_ref, *refs):
    qdo = refs[:peers]
    kv_refs = refs[peers : peers + pieces]
    outs = refs[peers + pieces : -3]
    stats_ref, dq_refs, part_refs = outs[0], outs[1 : peers + 1], outs[peers + 1 :]
    kv, sums, sems = refs[-3:]
    spans = []
    first = 0
    for ref in kv_refs:
        spans.append(pl.ds(first, ref.shape[0]))
        first += ref.shape[0]
    copies = run_copies([(ref, kv.at[span]) for ref, span in zip(kv_refs, spans)], sems)
    row_stats(me_ref[0], qdo, lse_ref, stats_ref)
    heads = (qdo[0].shape[0] - STAT) // KB
    sums[...] = jnp.zeros_like(sums)
    for copy in copies:
        copy.wait()
    for c in range(0, peers, 2):
        for h in range(heads):
            q, do = query_rows(qdo, c, h)
            slots = [slot_ref[(c // 2 * heads + h) * NSEL + n] for n in range(NSEL)]
            rows_kv = jnp.concatenate([kv[s] for s in slots], axis=0)
            k = rows_kv[:, :HD]
            v = rows_kv[:, HD:]
            lse_row = stats_ref[0, h : h + 1, c * KB : c * KB + QB]
            delta_row = stats_ref[1, h : h + 1, c * KB : c * KB + QB]
            prob = jnp.exp(dot(k, q, NT) * SCALE - lse_row)
            score = (prob * (dot(v, do, NT) - delta_row)).astype(jnp.bfloat16)
            dq = dot(score, k, TN) * SCALE
            cols = slice(h * HD, (h + 1) * HD)
            for i in range(2):
                dq_refs[c + i][:, cols] = dq[i * KB : (i + 1) * KB]
            dk = dot(score, q) * SCALE
            dv = dot(prob.astype(jnp.bfloat16), do)
            for n in range(NSEL):
                part = slice(n * KB, (n + 1) * KB)
                sums[slots[n], :, :HD] += dk[part]
                sums[slots[n], :, HD:] += dv[part]
    for part_ref, span in zip(part_refs, spans):
        part_ref[...] = sums[span].astype(part_ref.dtype)


def listed_terms(me, slots, lse, qdo, kv_pieces, part_types):
    peers = len(qdo)
    pieces = len(kv_pieces)
    units = sum(piece.shape[0] for piece in kv_pieces)
    whole = (units,) + kv_pieces[0].shape[1:]
    heads, tokens = lse.shape
    outs = pl.pallas_call(
        functools.partial(listed_kernel, peers, pieces),
        out_shape=(
            jax.ShapeDtypeStruct((2, heads, tokens), jnp.float32),
            *[jax.ShapeDtypeStruct((KB, heads * HD), jnp.float32)] * peers,
            *[jax.ShapeDtypeStruct(p.shape, kind) for p, kind in zip(kv_pieces, part_types)],
        ),
        in_specs=[SMEM, SMEM] + [VMEM] * (1 + peers) + [ANY] * pieces,
        out_specs=(VMEM,) * (1 + peers + pieces),
        scratch_shapes=[
            pltpu.VMEM(whole, jnp.bfloat16),
            pltpu.VMEM(whole, jnp.float32),
            pltpu.SemaphoreType.DMA((pieces,)),
        ],
        compiler_params=PARAMS,
        cost_estimate=pl.CostEstimate(
            flops=671_000_000, bytes_accessed=8_000_000, transcendentals=530_000
        ),
    )(me, slots, lse, *qdo, *kv_pieces)
    return outs[0], outs[1 : peers + 1], outs[peers + 1 :]


def add_kernel(*refs):
    *terms, out_ref = refs
    total = terms[0][...].astype(jnp.float32)
    for ref in terms[1:]:
        total = total + ref[...].astype(jnp.float32)
    out_ref[...] = total.astype(out_ref.dtype)


def add_rounded(*terms):
    return pl.pallas_call(
        add_kernel,
        out_shape=jax.ShapeDtypeStruct(terms[0].shape, jnp.bfloat16),
        in_specs=[VMEM] * len(terms),
        out_specs=VMEM,
        compiler_params=PARAMS,
    )(*terms)


def total_kernel(kv_heads, own_ref, *refs):
    peers = own_ref.shape[0] // kv_heads
    arrived, out_refs = refs[:-peers], refs[-peers:]
    for c, out_ref in enumerate(out_refs):
        part = slice(c * kv_heads, (c + 1) * kv_heads)
        total = own_ref[part]
        for ref in arrived:
            total = total + ref[part].astype(jnp.float32)
        out_ref[...] = total.astype(jnp.bfloat16)


def total_rounded(own, arrived, kv_heads):
    peers = own.shape[0] // kv_heads
    piece = jax.ShapeDtypeStruct((kv_heads,) + own.shape[1:], jnp.bfloat16)
    return pl.pallas_call(
        functools.partial(total_kernel, kv_heads),
        out_shape=(piece,) * peers,
        in_specs=[VMEM] * (1 + len(arrived)),
        out_specs=(VMEM,) * peers,
        compiler_params=PARAMS,
    )(own, *arrived)


def unpack_kernel(peers, me_ref, *refs):
    dq_refs, dkv_refs = refs[:peers], refs[peers : 2 * peers]
    gq_ref, gk_ref, gv_ref = refs[2 * peers :]
    width = dq_refs[0].shape[1]
    kv_heads = dkv_refs[0].shape[0]
    for c in range(peers):
        source = me_ref[0] ^ c
        gq_ref[:, lanes(source, width)] = dq_refs[c][...]
        for g in range(kv_heads):
            cols = lanes(source * kv_heads + g, HD)
            gk_ref[:, cols] = dkv_refs[c][g, :, :HD]
            gv_ref[:, cols] = dkv_refs[c][g, :, HD:]


def unpack(me, dq, dkv):
    peers = len(dq)
    tokens, width = dq[0].shape
    kv_width = dkv[0].shape[0] * peers * HD
    return pl.pallas_call(
        functools.partial(unpack_kernel, peers),
        out_shape=(
            jax.ShapeDtypeStruct((tokens, peers * width), jnp.bfloat16),
            jax.ShapeDtypeStruct((tokens, kv_width), jnp.bfloat16),
            jax.ShapeDtypeStruct((tokens, kv_width), jnp.bfloat16),
        ),
        in_specs=[SMEM] + [VMEM] * (2 * peers),
        out_specs=(VMEM,) * 3,
        compiler_params=PARAMS,
    )(me, *dq, *dkv)


def exchange(pieces):
    peers = len(pieces)
    moved = [
        lax.ppermute(pieces[c], "head", [(h, h ^ c) for h in range(peers)])
        for c in range(1, peers)
    ]
    return [pieces[0]] + moved


def body(queries, keys, values, outputs_saved, grad_out, lse, block_lists):
    peers = lax.axis_size("head")
    shards = lax.axis_size("seq")
    me = lax.axis_index("seq")
    head_me = lax.axis_index("head")
    me_ref = head_me.astype(jnp.int32).reshape(1)
    heads = lse.shape[1]
    kv_heads = heads // GROUP
    key_count = peers
    units = key_count * kv_heads

    own_kv = jnp.concatenate(exchange(pack_kv(me_ref, keys, values, peers)), axis=0)

    per_peer = block_lists.reshape(shards, -1)
    requests = per_peer.shape[1]
    order = jnp.arange(requests, dtype=jnp.int32)
    group_of = order % (heads * NSEL) // (NSEL * GROUP)
    block_turn = jnp.where(head_me >= peers // 2, requests // 2, 0)
    capacity = -(-requests // (shards - 1))
    dense = units <= capacity and shards == 8

    if dense:
        far = shards // 2
        swap = [(s, s ^ 1) for s in range(shards)]
        ahead = [(s, (s + 2) % shards) for s in range(shards)]
        back = [(s, (s - 2) % shards) for s in range(shards)]
        mine = lax.dynamic_index_in_dim(per_peer, me, 0, keepdims=False)
        owner = mine // key_count
        apart = (me // 2 - owner // 2) % far
        crossed = (me ^ owner) & 1
        piece = jnp.where(crossed == 1, far - 1 + (apart + 1) % far, apart - 1)
        slots = piece * units + (mine % key_count ^ head_me) * kv_heads + group_of
        slots = jnp.roll(slots, block_turn)
        later_me, own_kv, slots = lax.optimization_barrier((me_ref, own_kv, slots))
        q_pieces = list(pack_q(later_me, queries, grad_out, outputs_saved, peers))
        same1 = lax.ppermute(own_kv, "seq", ahead)
        cross0 = lax.ppermute(own_kv, "seq", swap)
        held, q_pieces[0] = lax.optimization_barrier((own_kv, q_pieces[0]))
        qdo = exchange(q_pieces)
        same3 = lax.ppermute(held, "seq", back)
        cross3 = lax.ppermute(cross0, "seq", back)
        same2 = lax.ppermute(same1, "seq", ahead)
        cross1 = lax.ppermute(same1, "seq", swap)
        held, cross1, qdo[1:] = lax.optimization_barrier((same2, cross1, qdo[1:]))
        cross2 = lax.ppermute(held, "seq", swap)
        kv_pieces = [same1, same2, same3, cross3, cross0, cross1, cross2]
        wide, low = jnp.float32, jnp.bfloat16
        part_types = [wide, wide, low, low, wide, low, low]
    else:
        owner = per_peer // key_count
        earlier = (owner[:, :, None] == owner[:, None, :]) & (order[None, :] < order[:, None])
        position = jnp.sum(earlier.astype(jnp.int32), axis=2)
        slots = lax.dynamic_index_in_dim(owner * capacity + position, me, 0, keepdims=False)
        hits = (owner == me)[:, :, None] & (position[:, :, None] == jnp.arange(capacity))
        hits = hits.astype(jnp.int32)
        used = jnp.sum(hits, axis=1).reshape(-1)
        wanted = (per_peer % key_count ^ head_me) * kv_heads + group_of[None, :]
        wanted = jnp.sum(hits * wanted[:, :, None], axis=1).reshape(-1)
        kv_pieces = [lax.all_to_all(own_kv[wanted], "seq", 0, 0, tiled=True)]
        part_types = [jnp.bfloat16]
        slots = jnp.roll(slots, block_turn)
        qdo = exchange(pack_q(me_ref, queries, grad_out, outputs_saved, peers))

    stats, listed, parts = listed_terms(me_ref, slots, lse.T, qdo, kv_pieces, part_types)
    dq, own = own_terms(me_ref, own_kv, stats, qdo, listed)

    if dense:
        stay1, stay2, away3, leave3, leave0, leave1, leave2 = parts
        came2 = lax.ppermute(leave2, "seq", swap)
        came3 = lax.ppermute(leave3, "seq", ahead)
        came1 = lax.ppermute(leave1, "seq", swap)
        hop = lax.ppermute(add_rounded(stay2, came2), "seq", back)
        away3, came3 = lax.optimization_barrier((away3, came3))
        turned = lax.ppermute(away3, "seq", ahead)
        near, came1 = lax.optimization_barrier((add_rounded(leave0, came3), came1))
        came0 = lax.ppermute(near, "seq", swap)
        hop, dq = lax.optimization_barrier((hop, list(dq)))
        side = add_rounded(stay1, came1, hop)
        arrived = [turned, came0, lax.ppermute(side, "seq", back)]
    else:
        parts = lax.all_to_all(parts[0], "seq", 0, 0, tiled=True)
        chosen = (jnp.arange(units)[:, None] == wanted[None, :]) & (used[None, :] > 0)
        total = jnp.dot(
            chosen.astype(jnp.bfloat16),
            parts.reshape(parts.shape[0], -1),
            preferred_element_type=jnp.float32,
        )
        arrived = [total.reshape(own.shape)]
    dq = exchange(dq)
    dkv = exchange(total_rounded(own, arrived, kv_heads))
    return unpack(me_ref, dq, dkv)


def solution(mesh):
    rows = P(("seq", "head"), None)
    in_specs = (rows, rows, rows, rows, rows, P("seq", "head"), P(None, "head", None))
    return jax.shard_map(
        body, mesh=mesh, in_specs=in_specs, out_specs=(rows, rows, rows), check_vma=False
    )
```

```python
import functools

import jax
import jax.numpy as jnp
from jax import lax
from jax.experimental import pallas as pl
from jax.experimental.pallas import tpu as pltpu
from jax.sharding import PartitionSpec as P

HD = 128
QB = 128
KB = 64
NSEL = 4
GROUP = 4
SCALE = HD ** (-0.5)
STAT = 16

VMEM = pl.BlockSpec(memory_space=pltpu.VMEM)
ANY = pl.BlockSpec(memory_space=pl.ANY)
HBM = pl.BlockSpec(memory_space=pltpu.HBM)
SMEM = pl.BlockSpec(memory_space=pltpu.SMEM)
NT = (((1,), (1,)), ((), ()))
TN = (((0,), (0,)), ((), ()))
PARAMS = pltpu.CompilerParams(vmem_limit_bytes=24 * 1024 * 1024)


def dot(a, b, dims=(((1,), (0,)), ((), ()))):
    return lax.dot_general(a, b, dims, preferred_element_type=jnp.float32)


def lanes(index, width):
    return pl.ds(pl.multiple_of(index * width, width), width)


def run_copies(pairs, sems):
    copies = [
        pltpu.make_async_copy(source, target, sems.at[i])
        for i, (source, target) in enumerate(pairs)
    ]
    for copy in copies:
        copy.start()
    return copies


def pack_kv_kernel(peers, me_ref, k_ref, v_ref, *refs):
    out_refs, sems = refs[:peers], refs[peers]
    kv_heads = out_refs[0].shape[0]
    pairs = []
    for c, out_ref in reversed(list(enumerate(out_refs))):
        for g in range(kv_heads):
            cols = lanes((me_ref[0] ^ c) * kv_heads + g, HD)
            pairs.append((k_ref.at[:, cols], out_ref.at[g, :, pl.ds(0, HD)]))
            pairs.append((v_ref.at[:, cols], out_ref.at[g, :, pl.ds(HD, HD)]))
    for copy in run_copies(pairs, sems):
        copy.wait()


def pack_kv(me, keys, values, peers):
    tokens, width = keys.shape
    kv_heads = width // HD // peers
    piece = jax.ShapeDtypeStruct((kv_heads, tokens, 2 * HD), jnp.bfloat16)
    return pl.pallas_call(
        functools.partial(pack_kv_kernel, peers),
        out_shape=(piece,) * peers,
        in_specs=[SMEM, HBM, HBM],
        out_specs=(VMEM,) * peers,
        scratch_shapes=[pltpu.SemaphoreType.DMA((2 * peers * kv_heads,))],
        compiler_params=PARAMS,
    )(me, keys, values)


def three_pieces(x):
    hi = x.astype(jnp.bfloat16)
    rest = x - hi.astype(jnp.float32)
    mid = rest.astype(jnp.bfloat16)
    low = (rest - mid.astype(jnp.float32)).astype(jnp.bfloat16)
    return hi, mid, low


def pack_q_kernel(peers, me_ref, q_any, do_any, o_any, *refs):
    half = peers // 2
    rows = refs[0].shape[0]
    out_refs = refs[:half] + tuple(refs[half].at[i * rows : (i + 1) * rows] for i in range(half))
    q_ref, do_ref, o_ref, sems = refs[half + 1 :]
    for copy in run_copies([(q_any, q_ref), (do_any, do_ref), (o_any, o_ref)], sems):
        copy.wait()
    heads = (out_refs[0].shape[0] - STAT) // KB
    lane = lax.broadcasted_iota(jnp.int32, (KB, HD), 1)
    delta = jnp.zeros((KB, HD), jnp.float32)
    for c, out_ref in enumerate(out_refs):
        for h in range(heads):
            cols = lanes((me_ref[0] ^ c) * heads + h, HD)
            do = do_ref[:, cols]
            out_ref[h * KB : (h + 1) * KB, :HD] = q_ref[:, cols]
            out_ref[h * KB : (h + 1) * KB, HD:] = do
            products = do.astype(jnp.float32) * o_ref[:, cols].astype(jnp.float32)
            total = jnp.sum(products, axis=-1, keepdims=True)
            delta = jnp.where(lane == c * heads + h, total, delta)
    by_head = delta.T
    for c, out_ref in enumerate(out_refs):
        hi, mid, low = three_pieces(by_head[c * heads : (c + 1) * heads])
        base = heads * KB
        zero = jnp.zeros((heads, HD - KB), jnp.bfloat16)
        first = jnp.concatenate([hi, zero, mid, zero], axis=1)
        second = jnp.concatenate([low, zero, zero, jnp.zeros_like(low)], axis=1)
        out_ref[base : base + STAT, :] = jnp.concatenate([first, second], axis=0)


def pack_q(me, queries, grad_out, outputs_saved, peers):
    tokens, width = queries.shape
    heads = width // HD // peers
    half = peers // 2
    rows = heads * tokens + STAT
    piece = jax.ShapeDtypeStruct((rows, 2 * HD), jnp.bfloat16)
    far = jax.ShapeDtypeStruct((half * rows, 2 * HD), jnp.bfloat16)
    return pl.pallas_call(
        functools.partial(pack_q_kernel, peers),
        out_shape=(piece,) * half + (far,),
        in_specs=[SMEM] + [HBM] * 3,
        out_specs=(VMEM,) * (half + 1),
        scratch_shapes=[pltpu.VMEM(queries.shape, jnp.bfloat16)] * 3
        + [pltpu.SemaphoreType.DMA((3,))],
        compiler_params=PARAMS,
    )(me, queries, grad_out, outputs_saved)


def query_rows(qdo, c, h):
    rows = slice(h * KB, (h + 1) * KB)
    pair = (qdo[c], qdo[c ^ 1])
    q = jnp.concatenate([ref[rows, :HD] for ref in pair], axis=0)
    do = jnp.concatenate([ref[rows, HD:] for ref in pair], axis=0)
    return q, do


def own_kernel(peers, me_ref, own_kv_ref, stats_ref, *refs):
    qdo = refs[:peers]
    listed_refs = refs[peers : 2 * peers]
    dq_refs, own_ref = refs[2 * peers : 3 * peers], refs[3 * peers]
    heads = (qdo[0].shape[0] - STAT) // KB
    kv_heads = heads // GROUP
    key_row = lax.broadcasted_iota(jnp.int32, (QB, QB), 0)
    query_row = lax.broadcasted_iota(jnp.int32, (QB, QB), 1)
    swapped = jnp.where((me_ref[0] & 1) == 1, KB, 0)
    causal = (key_row ^ swapped) <= (query_row ^ swapped)
    for c in range(0, peers, 2):
        for g in range(kv_heads):
            own = [(c + i) * kv_heads + g for i in range(2)]
            kv = jnp.concatenate([own_kv_ref[u] for u in own], axis=0)
            k = kv[:, :HD]
            v = kv[:, HD:]
            dk = jnp.zeros((QB, HD), jnp.float32)
            dv = jnp.zeros((QB, HD), jnp.float32)
            for h in range(g * GROUP, (g + 1) * GROUP):
                q, do = query_rows(qdo, c, h)
                lse_row = stats_ref[0, h : h + 1, c * KB : c * KB + QB]
                delta_row = stats_ref[1, h : h + 1, c * KB : c * KB + QB]
                prob = jnp.where(causal, jnp.exp(dot(k, q, NT) * SCALE - lse_row), 0.0)
                score = (prob * (dot(v, do, NT) - delta_row)).astype(jnp.bfloat16)
                dq = dot(score, k, TN) * SCALE
                cols = slice(h * HD, (h + 1) * HD)
                for i in range(2):
                    part = listed_refs[c + i][:, cols] + dq[i * KB : (i + 1) * KB]
                    dq_refs[c + i][:, cols] = part.astype(jnp.bfloat16)
                dk += dot(score, q)
                dv += dot(prob.astype(jnp.bfloat16), do)
            for i in range(2):
                own_ref[own[i], :, :HD] = dk[i * KB : (i + 1) * KB] * SCALE
                own_ref[own[i], :, HD:] = dv[i * KB : (i + 1) * KB]


def own_terms(me, own_kv, stats, qdo, listed):
    peers = len(qdo)
    piece = jax.ShapeDtypeStruct(listed[0].shape, jnp.bfloat16)
    outs = pl.pallas_call(
        functools.partial(own_kernel, peers),
        out_shape=(piece,) * peers + (jax.ShapeDtypeStruct(own_kv.shape, jnp.float32),),
        in_specs=[SMEM] + [VMEM] * (2 + 2 * peers),
        out_specs=(VMEM,) * (peers + 1),
        compiler_params=PARAMS,
        cost_estimate=pl.CostEstimate(
            flops=335_000_000, bytes_accessed=4_000_000, transcendentals=260_000
        ),
    )(me, own_kv, stats, *qdo, *listed)
    return outs[:peers], outs[peers]


def row_stats(me, qdo, lse_ref, stats_ref):
    peers = len(qdo)
    heads = (qdo[0].shape[0] - STAT) // KB
    base = heads * KB
    lse_blocks = [lse_ref[:, c * KB : (c + 1) * KB] for c in range(peers)]
    for c in range(peers):
        first = qdo[c][base : base + heads, :].astype(jnp.float32)
        second = qdo[c][base + heads : base + 2 * heads, :].astype(jnp.float32)
        delta = first[:, :KB] + first[:, HD : HD + KB] + second[:, :KB]
        lse_here = lse_blocks[0]
        for t in range(1, peers):
            lse_here = jnp.where((me ^ c) == t, lse_blocks[t], lse_here)
        stats_ref[0, :, c * KB : (c + 1) * KB] = lse_here
        stats_ref[1, :, c * KB : (c + 1) * KB] = delta


def listed_kernel(peers, pieces, me_ref, slot_ref, lse_ref, *refs):
    qdo = refs[:peers]
    kv_refs = refs[peers : peers + pieces]
    outs = refs[peers + pieces : -3]
    stats_ref, dq_refs, part_refs = outs[0], outs[1 : peers + 1], outs[peers + 1 :]
    kv, sums, sems = refs[-3:]
    spans = []
    first = 0
    for ref in kv_refs:
        spans.append(pl.ds(first, ref.shape[0]))
        first += ref.shape[0]
    copies = run_copies([(ref, kv.at[span]) for ref, span in zip(kv_refs, spans)], sems)
    row_stats(me_ref[0], qdo, lse_ref, stats_ref)
    heads = (qdo[0].shape[0] - STAT) // KB
    sums[...] = jnp.zeros_like(sums)
    for copy in copies:
        copy.wait()
    for c in range(0, peers, 2):
        for h in range(heads):
            q, do = query_rows(qdo, c, h)
            slots = [slot_ref[(c // 2 * heads + h) * NSEL + n] for n in range(NSEL)]
            rows_kv = jnp.concatenate([kv[s] for s in slots], axis=0)
            k = rows_kv[:, :HD]
            v = rows_kv[:, HD:]
            lse_row = stats_ref[0, h : h + 1, c * KB : c * KB + QB]
            delta_row = stats_ref[1, h : h + 1, c * KB : c * KB + QB]
            prob = jnp.exp(dot(k, q, NT) * SCALE - lse_row)
            score = (prob * (dot(v, do, NT) - delta_row)).astype(jnp.bfloat16)
            dq = dot(score, k, TN) * SCALE
            cols = slice(h * HD, (h + 1) * HD)
            for i in range(2):
                dq_refs[c + i][:, cols] = dq[i * KB : (i + 1) * KB]
            dk = dot(score, q) * SCALE
            dv = dot(prob.astype(jnp.bfloat16), do)
            for n in range(NSEL):
                part = slice(n * KB, (n + 1) * KB)
                sums[slots[n], :, :HD] += dk[part]
                sums[slots[n], :, HD:] += dv[part]
    for part_ref, span in zip(part_refs, spans):
        part_ref[...] = sums[span].astype(part_ref.dtype)


def listed_terms(me, slots, lse, qdo, kv_pieces, part_types):
    peers = len(qdo)
    pieces = len(kv_pieces)
    units = sum(piece.shape[0] for piece in kv_pieces)
    whole = (units,) + kv_pieces[0].shape[1:]
    heads, tokens = lse.shape
    outs = pl.pallas_call(
        functools.partial(listed_kernel, peers, pieces),
        out_shape=(
            jax.ShapeDtypeStruct((2, heads, tokens), jnp.float32),
            *[jax.ShapeDtypeStruct((KB, heads * HD), jnp.float32)] * peers,
            *[jax.ShapeDtypeStruct(p.shape, kind) for p, kind in zip(kv_pieces, part_types)],
        ),
        in_specs=[SMEM, SMEM] + [VMEM] * (1 + peers) + [ANY] * pieces,
        out_specs=(VMEM,) * (1 + peers + pieces),
        scratch_shapes=[
            pltpu.VMEM(whole, jnp.bfloat16),
            pltpu.VMEM(whole, jnp.float32),
            pltpu.SemaphoreType.DMA((pieces,)),
        ],
        compiler_params=PARAMS,
        cost_estimate=pl.CostEstimate(
            flops=671_000_000, bytes_accessed=8_000_000, transcendentals=530_000
        ),
    )(me, slots, lse, *qdo, *kv_pieces)
    return outs[0], outs[1 : peers + 1], outs[peers + 1 :]


def add_kernel(*refs):
    *terms, out_ref = refs
    total = terms[0][...].astype(jnp.float32)
    for ref in terms[1:]:
        total = total + ref[...].astype(jnp.float32)
    out_ref[...] = total.astype(out_ref.dtype)


def add_rounded(*terms):
    return pl.pallas_call(
        add_kernel,
        out_shape=jax.ShapeDtypeStruct(terms[0].shape, jnp.bfloat16),
        in_specs=[VMEM] * len(terms),
        out_specs=VMEM,
        compiler_params=PARAMS,
    )(*terms)


def add_blocks_kernel(terms, *refs):
    term_refs, out_refs = refs[:terms], refs[terms:]
    for c, out_ref in enumerate(out_refs):
        size = out_ref.shape[0]
        part = slice(c * size, (c + 1) * size)
        total = term_refs[0][part].astype(jnp.float32)
        for ref in term_refs[1:]:
            total = total + ref[part].astype(jnp.float32)
        out_ref[...] = total.astype(out_ref.dtype)


def add_blocks(kv_heads, *terms):
    peers = terms[0].shape[0] // kv_heads
    piece = jax.ShapeDtypeStruct((kv_heads,) + terms[0].shape[1:], jnp.bfloat16)
    return pl.pallas_call(
        functools.partial(add_blocks_kernel, len(terms)),
        out_shape=(piece,) * peers,
        in_specs=[VMEM] * len(terms),
        out_specs=(VMEM,) * peers,
        compiler_params=PARAMS,
    )(*terms)


def unpack_kernel(peers, sets, me_ref, *refs):
    dq_refs, dkv_refs = refs[:peers], refs[peers : peers * (1 + sets)]
    gq_ref, gk_ref, gv_ref = refs[peers * (1 + sets) :]
    width = dq_refs[0].shape[1]
    kv_heads = dkv_refs[0].shape[0]
    for c in range(peers):
        source = me_ref[0] ^ c
        gq_ref[:, lanes(source, width)] = dq_refs[c][...]
        for g in range(kv_heads):
            cols = lanes(source * kv_heads + g, HD)
            total = dkv_refs[c][g].astype(jnp.float32)
            for i in range(1, sets):
                total = total + dkv_refs[i * peers + c][g].astype(jnp.float32)
            total = total.astype(jnp.bfloat16)
            gk_ref[:, cols] = total[:, :HD]
            gv_ref[:, cols] = total[:, HD:]


def unpack(me, dq, dkv):
    peers = len(dq)
    tokens, width = dq[0].shape
    kv_width = dkv[0][0].shape[0] * peers * HD
    flat = [piece for pieces in dkv for piece in pieces]
    return pl.pallas_call(
        functools.partial(unpack_kernel, peers, len(dkv)),
        out_shape=(
            jax.ShapeDtypeStruct((tokens, peers * width), jnp.bfloat16),
            jax.ShapeDtypeStruct((tokens, kv_width), jnp.bfloat16),
            jax.ShapeDtypeStruct((tokens, kv_width), jnp.bfloat16),
        ),
        in_specs=[SMEM] + [VMEM] * (peers + len(flat)),
        out_specs=(VMEM,) * 3,
        compiler_params=PARAMS,
    )(me, *dq, *flat)


def exchange(pieces):
    peers = len(pieces)
    moved = [
        lax.ppermute(pieces[c], "head", [(h, h ^ c) for h in range(peers)])
        for c in range(1, peers)
    ]
    return [pieces[0]] + moved


def exchange_rows(here, near, far):
    rows = here.shape[0]
    flip = [(h, h ^ 1) for h in range(4)]
    across = [(h, h ^ 2) for h in range(4)]
    far = lax.ppermute(far, "head", across)
    near = lax.ppermute(near, "head", flip)
    return [here, near, far[:rows], lax.ppermute(far[rows:], "head", flip)]


def body(queries, keys, values, outputs_saved, grad_out, lse, block_lists):
    peers = lax.axis_size("head")
    shards = lax.axis_size("seq")
    me = lax.axis_index("seq")
    head_me = lax.axis_index("head")
    me_ref = head_me.astype(jnp.int32).reshape(1)
    heads = lse.shape[1]
    kv_heads = heads // GROUP
    key_count = peers
    units = key_count * kv_heads

    kv_pack = pack_kv(me_ref, keys, values, peers)
    own_kv = jnp.concatenate(exchange(kv_pack), axis=0)

    per_peer = block_lists.reshape(shards, -1)
    requests = per_peer.shape[1]
    order = jnp.arange(requests, dtype=jnp.int32)
    group_of = order % (heads * NSEL) // (NSEL * GROUP)
    block_turn = jnp.where(head_me >= peers // 2, requests // 2, 0)
    capacity = -(-requests // (shards - 1))
    dense = units <= capacity and shards == 8

    if dense:
        far = shards // 2
        swap = [(s, s ^ 1) for s in range(shards)]
        ahead = [(s, (s + 2) % shards) for s in range(shards)]
        back = [(s, (s - 2) % shards) for s in range(shards)]
        later_me, _ = lax.optimization_barrier((me_ref, kv_pack))
        q_pieces = pack_q(later_me, queries, grad_out, outputs_saved, peers)
        own_kv, q_pieces = lax.optimization_barrier((own_kv, q_pieces))
        qdo = exchange_rows(*q_pieces)
        same1 = lax.ppermute(own_kv, "seq", ahead)
        cross0 = lax.ppermute(own_kv, "seq", swap)
        same3 = lax.ppermute(own_kv, "seq", back)
        same2 = lax.ppermute(same1, "seq", ahead)
        cross1 = lax.ppermute(same1, "seq", swap)
        cross3 = lax.ppermute(same3, "seq", swap)
        held, cross0, cross1 = lax.optimization_barrier((same2, cross0, cross1))
        cross2 = lax.ppermute(held, "seq", swap)
        per_peer, cross0 = lax.optimization_barrier((per_peer, cross0))
        mine = lax.dynamic_index_in_dim(per_peer, me, 0, keepdims=False)
        owner = mine // key_count
        apart = (me // 2 - owner // 2) % far
        crossed = (me ^ owner) & 1
        piece = jnp.where(crossed == 1, far - 1 + (apart + 1) % far, apart - 1)
        slots = piece * units + (mine % key_count ^ head_me) * kv_heads + group_of
        slots = jnp.roll(slots, block_turn)
        kv_pieces = [same1, same2, same3, cross3, cross0, cross1, cross2]
        wide, low = jnp.float32, jnp.bfloat16
        part_types = [wide, wide, low, low, wide, low, low]
    else:
        owner = per_peer // key_count
        earlier = (owner[:, :, None] == owner[:, None, :]) & (order[None, :] < order[:, None])
        position = jnp.sum(earlier.astype(jnp.int32), axis=2)
        slots = lax.dynamic_index_in_dim(owner * capacity + position, me, 0, keepdims=False)
        hits = (owner == me)[:, :, None] & (position[:, :, None] == jnp.arange(capacity))
        hits = hits.astype(jnp.int32)
        used = jnp.sum(hits, axis=1).reshape(-1)
        wanted = (per_peer % key_count ^ head_me) * kv_heads + group_of[None, :]
        wanted = jnp.sum(hits * wanted[:, :, None], axis=1).reshape(-1)
        kv_pieces = [lax.all_to_all(own_kv[wanted], "seq", 0, 0, tiled=True)]
        part_types = [jnp.bfloat16]
        slots = jnp.roll(slots, block_turn)
        qdo = exchange_rows(*pack_q(me_ref, queries, grad_out, outputs_saved, peers))

    stats, listed, parts = listed_terms(me_ref, slots, lse.T, qdo, kv_pieces, part_types)
    dq, own = own_terms(me_ref, own_kv, stats, qdo, listed)

    if dense:
        stay1, stay2, away3, leave3, leave0, leave1, leave2 = parts
        came3 = lax.ppermute(jnp.concatenate([leave3, away3], axis=0), "seq", ahead)
        came2 = lax.ppermute(leave2, "seq", swap)
        came1 = lax.ppermute(leave1, "seq", swap)
        hop = lax.ppermute(add_rounded(stay2, came2), "seq", back)
        came3, dq = lax.optimization_barrier((came3, list(dq)))
        dq = exchange(dq)
        near, came1 = lax.optimization_barrier((add_rounded(leave0, came3[:units]), came1))
        came0 = lax.ppermute(near, "seq", swap)
        side = lax.ppermute(add_rounded(stay1, came1, hop), "seq", back)
        dkv = [exchange(add_blocks(kv_heads, own, came3[units:], came0, side))]
    else:
        parts = lax.all_to_all(parts[0], "seq", 0, 0, tiled=True)
        chosen = (jnp.arange(units)[:, None] == wanted[None, :]) & (used[None, :] > 0)
        total = jnp.dot(
            chosen.astype(jnp.bfloat16),
            parts.reshape(parts.shape[0], -1),
            preferred_element_type=jnp.float32,
        )
        dq = exchange(dq)
        dkv = [exchange(add_blocks(kv_heads, own, total.reshape(own.shape)))]
    return unpack(me_ref, dq, dkv)


def solution(mesh):
    rows = P(("seq", "head"), None)
    in_specs = (rows, rows, rows, rows, rows, P("seq", "head"), P(None, "head", None))
    return jax.shard_map(
        body, mesh=mesh, in_specs=in_specs, out_specs=(rows, rows, rows), check_vma=False
    )
```

```python
import functools

import jax
import jax.numpy as jnp
from jax import lax
from jax.experimental import pallas as pl
from jax.experimental.pallas import tpu as pltpu
from jax.sharding import PartitionSpec as P

HD = 128
QB = 128
KB = 64
NSEL = 4
GROUP = 4
SCALE = HD ** (-0.5)
STAT = 16

VMEM = pl.BlockSpec(memory_space=pltpu.VMEM)
ANY = pl.BlockSpec(memory_space=pl.ANY)
HBM = pl.BlockSpec(memory_space=pltpu.HBM)
SMEM = pl.BlockSpec(memory_space=pltpu.SMEM)
NT = (((1,), (1,)), ((), ()))
TN = (((0,), (0,)), ((), ()))
PACK_PARAMS = pltpu.CompilerParams(vmem_limit_bytes=60 * 1024 * 1024)
PARAMS = pltpu.CompilerParams(vmem_limit_bytes=24 * 1024 * 1024)


def dot(a, b, dims=(((1,), (0,)), ((), ()))):
    return lax.dot_general(a, b, dims, preferred_element_type=jnp.float32)


def lanes(index, width):
    return pl.ds(pl.multiple_of(index * width, width), width)


def run_copies(pairs, sems):
    copies = [
        pltpu.make_async_copy(source, target, sems.at[i])
        for i, (source, target) in enumerate(pairs)
    ]
    for copy in copies:
        copy.start()
    return copies


def pack_kv_kernel(peers, me_ref, k_ref, v_ref, *refs):
    out_refs, sems = refs[:peers], refs[peers]
    kv_heads = out_refs[0].shape[0]
    pairs = []
    for c, out_ref in reversed(list(enumerate(out_refs))):
        for g in range(kv_heads):
            cols = lanes((me_ref[0] ^ c) * kv_heads + g, HD)
            pairs.append((k_ref.at[:, cols], out_ref.at[g, :, pl.ds(0, HD)]))
            pairs.append((v_ref.at[:, cols], out_ref.at[g, :, pl.ds(HD, HD)]))
    for copy in run_copies(pairs, sems):
        copy.wait()


def pack_kv(me, keys, values, peers):
    tokens, width = keys.shape
    kv_heads = width // HD // peers
    piece = jax.ShapeDtypeStruct((kv_heads, tokens, 2 * HD), jnp.bfloat16)
    return pl.pallas_call(
        functools.partial(pack_kv_kernel, peers),
        out_shape=(piece,) * peers,
        in_specs=[SMEM, HBM, HBM],
        out_specs=(VMEM,) * peers,
        scratch_shapes=[pltpu.SemaphoreType.DMA((2 * peers * kv_heads,))],
        compiler_params=PACK_PARAMS,
    )(me, keys, values)


def three_pieces(x):
    hi = x.astype(jnp.bfloat16)
    rest = x - hi.astype(jnp.float32)
    mid = rest.astype(jnp.bfloat16)
    low = (rest - mid.astype(jnp.float32)).astype(jnp.bfloat16)
    return hi, mid, low


def pack_q_kernel(peers, me_ref, q_any, do_any, o_any, *refs):
    half = peers // 2
    rows = refs[0].shape[0]
    out_refs = refs[:half] + tuple(refs[half].at[i * rows : (i + 1) * rows] for i in range(half))
    q_ref, do_ref, o_ref, sems = refs[half + 1 :]
    for copy in run_copies([(q_any, q_ref), (do_any, do_ref), (o_any, o_ref)], sems):
        copy.wait()
    heads = (out_refs[0].shape[0] - STAT) // KB
    lane = lax.broadcasted_iota(jnp.int32, (KB, HD), 1)
    delta = jnp.zeros((KB, HD), jnp.float32)
    for c, out_ref in enumerate(out_refs):
        for h in range(heads):
            cols = lanes((me_ref[0] ^ c) * heads + h, HD)
            do = do_ref[:, cols]
            out_ref[h * KB : (h + 1) * KB, :HD] = q_ref[:, cols]
            out_ref[h * KB : (h + 1) * KB, HD:] = do
            products = do.astype(jnp.float32) * o_ref[:, cols].astype(jnp.float32)
            total = jnp.sum(products, axis=-1, keepdims=True)
            delta = jnp.where(lane == c * heads + h, total, delta)
    by_head = delta.T
    for c, out_ref in enumerate(out_refs):
        hi, mid, low = three_pieces(by_head[c * heads : (c + 1) * heads])
        base = heads * KB
        zero = jnp.zeros((heads, HD - KB), jnp.bfloat16)
        first = jnp.concatenate([hi, zero, mid, zero], axis=1)
        second = jnp.concatenate([low, zero, zero, jnp.zeros_like(low)], axis=1)
        out_ref[base : base + STAT, :] = jnp.concatenate([first, second], axis=0)


def pack_q(me, queries, grad_out, outputs_saved, peers):
    tokens, width = queries.shape
    heads = width // HD // peers
    half = peers // 2
    rows = heads * tokens + STAT
    piece = jax.ShapeDtypeStruct((rows, 2 * HD), jnp.bfloat16)
    far = jax.ShapeDtypeStruct((half * rows, 2 * HD), jnp.bfloat16)
    return pl.pallas_call(
        functools.partial(pack_q_kernel, peers),
        out_shape=(piece,) * half + (far,),
        in_specs=[SMEM] + [HBM] * 3,
        out_specs=(VMEM,) * (half + 1),
        scratch_shapes=[pltpu.VMEM(queries.shape, jnp.bfloat16)] * 3
        + [pltpu.SemaphoreType.DMA((3,))],
        compiler_params=PACK_PARAMS,
    )(me, queries, grad_out, outputs_saved)


def query_rows(qdo, c, h):
    rows = slice(h * KB, (h + 1) * KB)
    pair = (qdo[c], qdo[c ^ 1])
    q = jnp.concatenate([ref[rows, :HD] for ref in pair], axis=0)
    do = jnp.concatenate([ref[rows, HD:] for ref in pair], axis=0)
    return q, do


def own_kernel(peers, me_ref, own_kv_ref, stats_ref, *refs):
    qdo = refs[:peers]
    listed_refs = refs[peers : 2 * peers]
    dq_refs, own_ref = refs[2 * peers : 3 * peers], refs[3 * peers]
    heads = (qdo[0].shape[0] - STAT) // KB
    kv_heads = heads // GROUP
    key_row = lax.broadcasted_iota(jnp.int32, (QB, QB), 0)
    query_row = lax.broadcasted_iota(jnp.int32, (QB, QB), 1)
    swapped = jnp.where((me_ref[0] & 1) == 1, KB, 0)
    causal = (key_row ^ swapped) <= (query_row ^ swapped)
    for c in range(0, peers, 2):
        for g in range(kv_heads):
            own = [(c + i) * kv_heads + g for i in range(2)]
            kv = jnp.concatenate([own_kv_ref[u] for u in own], axis=0)
            k = kv[:, :HD]
            v = kv[:, HD:]
            dk = jnp.zeros((QB, HD), jnp.float32)
            dv = jnp.zeros((QB, HD), jnp.float32)
            for h in range(g * GROUP, (g + 1) * GROUP):
                q, do = query_rows(qdo, c, h)
                lse_row = stats_ref[0, h : h + 1, c * KB : c * KB + QB]
                delta_row = stats_ref[1, h : h + 1, c * KB : c * KB + QB]
                prob = jnp.where(causal, jnp.exp(dot(k, q, NT) * SCALE - lse_row), 0.0)
                score = (prob * (dot(v, do, NT) - delta_row)).astype(jnp.bfloat16)
                dq = dot(score, k, TN) * SCALE
                cols = slice(h * HD, (h + 1) * HD)
                for i in range(2):
                    part = listed_refs[c + i][:, cols] + dq[i * KB : (i + 1) * KB]
                    dq_refs[c + i][:, cols] = part.astype(jnp.bfloat16)
                dk += dot(score, q)
                dv += dot(prob.astype(jnp.bfloat16), do)
            for i in range(2):
                own_ref[own[i], :, :HD] = dk[i * KB : (i + 1) * KB] * SCALE
                own_ref[own[i], :, HD:] = dv[i * KB : (i + 1) * KB]


def own_terms(me, own_kv, stats, qdo, listed):
    peers = len(qdo)
    piece = jax.ShapeDtypeStruct(listed[0].shape, jnp.bfloat16)
    outs = pl.pallas_call(
        functools.partial(own_kernel, peers),
        out_shape=(piece,) * peers + (jax.ShapeDtypeStruct(own_kv.shape, jnp.float32),),
        in_specs=[SMEM] + [VMEM] * (2 + 2 * peers),
        out_specs=(VMEM,) * (peers + 1),
        compiler_params=PARAMS,
        cost_estimate=pl.CostEstimate(
            flops=335_000_000, bytes_accessed=4_000_000, transcendentals=260_000
        ),
    )(me, own_kv, stats, *qdo, *listed)
    return outs[:peers], outs[peers]


def row_stats(me, qdo, lse_ref, stats_ref):
    peers = len(qdo)
    heads = (qdo[0].shape[0] - STAT) // KB
    base = heads * KB
    lse_blocks = [lse_ref[:, c * KB : (c + 1) * KB] for c in range(peers)]
    for c in range(peers):
        first = qdo[c][base : base + heads, :].astype(jnp.float32)
        second = qdo[c][base + heads : base + 2 * heads, :].astype(jnp.float32)
        delta = first[:, :KB] + first[:, HD : HD + KB] + second[:, :KB]
        lse_here = lse_blocks[0]
        for t in range(1, peers):
            lse_here = jnp.where((me ^ c) == t, lse_blocks[t], lse_here)
        stats_ref[0, :, c * KB : (c + 1) * KB] = lse_here
        stats_ref[1, :, c * KB : (c + 1) * KB] = delta


def listed_kernel(peers, me_ref, slot_ref, lse_ref, kv, *refs):
    qdo, outs, sums = refs[:peers], refs[peers:-1], refs[-1]
    stats_ref, dq_refs, part_refs = outs[0], outs[1 : peers + 1], outs[peers + 1 :]
    row_stats(me_ref[0], qdo, lse_ref, stats_ref)
    heads = (qdo[0].shape[0] - STAT) // KB
    sums[...] = jnp.zeros_like(sums)

    def scores(c, h):
        q, do = query_rows(qdo, c, h)
        slots = [slot_ref[(c // 2 * heads + h) * NSEL + n] for n in range(NSEL)]
        rows_kv = jnp.concatenate([kv[s] for s in slots], axis=0)
        k = rows_kv[:, :HD]
        v = rows_kv[:, HD:]
        lse_row = stats_ref[0, h : h + 1, c * KB : c * KB + QB]
        delta_row = stats_ref[1, h : h + 1, c * KB : c * KB + QB]
        prob = jnp.exp(dot(k, q, NT) * SCALE - lse_row)
        score = (prob * (dot(v, do, NT) - delta_row)).astype(jnp.bfloat16)
        return c, h, slots, q, do, k, prob.astype(jnp.bfloat16), score

    def gradients(c, h, slots, q, do, k, prob, score):
        dq = dot(score, k, TN) * SCALE
        cols = slice(h * HD, (h + 1) * HD)
        for i in range(2):
            dq_refs[c + i][:, cols] = dq[i * KB : (i + 1) * KB]
        dk = dot(score, q) * SCALE
        dv = dot(prob, do)
        for n in range(NSEL):
            part = slice(n * KB, (n + 1) * KB)
            sums[slots[n], :, :HD] += dk[part]
            sums[slots[n], :, HD:] += dv[part]

    waiting = []
    for c in range(0, peers, 2):
        for h in range(heads):
            waiting.append(scores(c, h))
            if len(waiting) > 2:
                gradients(*waiting.pop(0))
    for state in waiting:
        gradients(*state)
    first = 0
    for part_ref in part_refs:
        part_ref[...] = sums[first : first + part_ref.shape[0]].astype(part_ref.dtype)
        first += part_ref.shape[0]


def listed_terms(me, slots, lse, kv, qdo, parts):
    peers = len(qdo)
    heads, tokens = lse.shape
    outs = pl.pallas_call(
        functools.partial(listed_kernel, peers),
        out_shape=(
            jax.ShapeDtypeStruct((2, heads, tokens), jnp.float32),
            *[jax.ShapeDtypeStruct((KB, heads * HD), jnp.float32)] * peers,
            *[jax.ShapeDtypeStruct((units,) + kv.shape[1:], kind) for units, kind in parts],
        ),
        in_specs=[SMEM, SMEM] + [VMEM] * (2 + peers),
        out_specs=(VMEM,) * (1 + peers + len(parts)),
        scratch_shapes=[pltpu.VMEM(kv.shape, jnp.float32)],
        compiler_params=PARAMS,
        cost_estimate=pl.CostEstimate(
            flops=671_000_000, bytes_accessed=8_000_000, transcendentals=530_000
        ),
    )(me, slots, lse, kv, *qdo)
    return outs[0], outs[1 : peers + 1], outs[peers + 1 :]


def add_kernel(firsts, *refs):
    terms, out_refs = refs[: len(firsts)], refs[len(firsts) :]
    done = 0
    for out_ref in out_refs:
        size = out_ref.shape[0]
        total = None
        for ref, first in zip(terms, firsts):
            part = ref[first + done : first + done + size].astype(jnp.float32)
            total = part if total is None else total + part
        out_ref[...] = total.astype(out_ref.dtype)
        done += size


def add_rounded(units, *terms, cuts=1):
    terms = [term if isinstance(term, tuple) else (term, 0) for term in terms]
    arrays = [array for array, _ in terms]
    piece = jax.ShapeDtypeStruct((units // cuts,) + arrays[0].shape[1:], jnp.bfloat16)
    outs = pl.pallas_call(
        functools.partial(add_kernel, [first for _, first in terms]),
        out_shape=(piece,) * cuts,
        in_specs=[VMEM] * len(arrays),
        out_specs=(VMEM,) * cuts,
        compiler_params=PARAMS,
    )(*arrays)
    return outs if cuts > 1 else outs[0]


def unpack_kernel(peers, me_ref, *refs):
    dq_refs, dkv_refs = refs[:peers], refs[peers : 2 * peers]
    gq_ref, gk_ref, gv_ref = refs[2 * peers :]
    width = dq_refs[0].shape[1]
    kv_heads = dkv_refs[0].shape[0]
    for c in range(peers):
        source = me_ref[0] ^ c
        gq_ref[:, lanes(source, width)] = dq_refs[c][...]
        for g in range(kv_heads):
            cols = lanes(source * kv_heads + g, HD)
            gk_ref[:, cols] = dkv_refs[c][g, :, :HD]
            gv_ref[:, cols] = dkv_refs[c][g, :, HD:]


def unpack(me, dq, dkv):
    peers = len(dq)
    tokens, width = dq[0].shape
    kv_width = dkv[0].shape[0] * peers * HD
    return pl.pallas_call(
        functools.partial(unpack_kernel, peers),
        out_shape=(
            jax.ShapeDtypeStruct((tokens, peers * width), jnp.bfloat16),
            jax.ShapeDtypeStruct((tokens, kv_width), jnp.bfloat16),
            jax.ShapeDtypeStruct((tokens, kv_width), jnp.bfloat16),
        ),
        in_specs=[SMEM] + [VMEM] * (2 * peers),
        out_specs=(VMEM,) * 3,
        compiler_params=PARAMS,
    )(me, *dq, *dkv)


def exchange(pieces):
    peers = len(pieces)
    moved = [
        lax.ppermute(pieces[c], "head", [(h, h ^ c) for h in range(peers)])
        for c in range(1, peers)
    ]
    return [pieces[0]] + moved


def exchange_rows(here, near, far):
    rows = here.shape[0]
    flip = [(h, h ^ 1) for h in range(4)]
    across = [(h, h ^ 2) for h in range(4)]
    far = lax.ppermute(far, "head", across)
    near = lax.ppermute(near, "head", flip)
    return [here, near, far[:rows], lax.ppermute(far[rows:], "head", flip)]


def body(queries, keys, values, outputs_saved, grad_out, lse, block_lists):
    peers = lax.axis_size("head")
    shards = lax.axis_size("seq")
    me = lax.axis_index("seq")
    head_me = lax.axis_index("head")
    me_ref = head_me.astype(jnp.int32).reshape(1)
    heads = lse.shape[1]
    kv_heads = heads // GROUP
    key_count = peers
    units = key_count * kv_heads

    kv_pack = pack_kv(me_ref, keys, values, peers)
    own_kv = jnp.concatenate(exchange(kv_pack), axis=0)

    per_peer = block_lists.reshape(shards, -1)
    requests = per_peer.shape[1]
    order = jnp.arange(requests, dtype=jnp.int32)
    group_of = order % (heads * NSEL) // (NSEL * GROUP)
    block_turn = jnp.where(head_me >= peers // 2, requests // 2, 0)
    capacity = -(-requests // (shards - 1))
    dense = units <= capacity and shards == 8

    if dense:
        far = shards // 2
        swap = [(s, s ^ 1) for s in range(shards)]
        ahead = [(s, (s + 2) % shards) for s in range(shards)]
        back = [(s, (s - 2) % shards) for s in range(shards)]
        later_me, _ = lax.optimization_barrier((me_ref, kv_pack))
        q_pieces = pack_q(later_me, queries, grad_out, outputs_saved, peers)
        own_kv, q_pieces, per_peer = lax.optimization_barrier((own_kv, q_pieces, per_peer))
        mine = lax.dynamic_index_in_dim(per_peer, me, 0, keepdims=False)
        owner = mine // key_count
        apart = (me // 2 - owner // 2) % far
        crossed = (me ^ owner) & 1
        piece = jnp.where(crossed == 1, far - 1 + (apart + 1) % far, apart - 1)
        slots = piece * units + (mine % key_count ^ head_me) * kv_heads + group_of
        slots = jnp.roll(slots, block_turn)
        q_pieces, slots = lax.optimization_barrier((q_pieces, slots))
        qdo = exchange_rows(*q_pieces)
        same1 = lax.ppermute(own_kv, "seq", ahead)
        cross0 = lax.ppermute(own_kv, "seq", swap)
        same3 = lax.ppermute(own_kv, "seq", back)
        same2 = lax.ppermute(same1, "seq", ahead)
        cross1 = lax.ppermute(same1, "seq", swap)
        cross3 = lax.ppermute(same3, "seq", swap)
        held, cross1 = lax.optimization_barrier((same2, cross1))
        cross2 = lax.ppermute(held, "seq", swap)
        kv_all = jnp.zeros((7 * units,) + own_kv.shape[1:], jnp.bfloat16)
        arriving = [(same1, 0), (cross0, 4), (cross1, 5), (same2, 1), (same3, 2)]
        for array, at in arriving + [(cross2, 6), (cross3, 3)]:
            kv_all = lax.dynamic_update_slice_in_dim(kv_all, array, at * units, 0)
        wide, low = jnp.float32, jnp.bfloat16
        part_types = [(1, wide), (1, wide), (2, low), (1, wide), (1, low), (1, low)]
        part_types = [(count * units, kind) for count, kind in part_types]
    else:
        owner = per_peer // key_count
        earlier = (owner[:, :, None] == owner[:, None, :]) & (order[None, :] < order[:, None])
        position = jnp.sum(earlier.astype(jnp.int32), axis=2)
        slots = lax.dynamic_index_in_dim(owner * capacity + position, me, 0, keepdims=False)
        hits = (owner == me)[:, :, None] & (position[:, :, None] == jnp.arange(capacity))
        hits = hits.astype(jnp.int32)
        used = jnp.sum(hits, axis=1).reshape(-1)
        wanted = (per_peer % key_count ^ head_me) * kv_heads + group_of[None, :]
        wanted = jnp.sum(hits * wanted[:, :, None], axis=1).reshape(-1)
        kv_all = lax.all_to_all(own_kv[wanted], "seq", 0, 0, tiled=True)
        part_types = [(kv_all.shape[0], jnp.bfloat16)]
        slots = jnp.roll(slots, block_turn)
        qdo = exchange_rows(*pack_q(me_ref, queries, grad_out, outputs_saved, peers))

    stats, listed, parts = listed_terms(me_ref, slots, lse.T, kv_all, qdo, part_types)
    dq, own = own_terms(me_ref, own_kv, stats, qdo, listed)

    if dense:
        stay1, stay2, away3, leave0, leave1, leave2 = parts
        came2 = lax.ppermute(leave2, "seq", swap)
        came3 = lax.ppermute(away3, "seq", ahead)
        came1 = lax.ppermute(leave1, "seq", swap)
        hop = lax.ppermute(add_rounded(units, stay2, came2), "seq", back)
        came3, dq = lax.optimization_barrier((came3, list(dq)))
        dq = exchange(dq)
        near, came1 = lax.optimization_barrier((add_rounded(units, leave0, (came3, units)), came1))
        came0 = lax.ppermute(near, "seq", swap)
        side = lax.ppermute(add_rounded(units, stay1, came1, hop), "seq", back)
        dkv = exchange(add_rounded(units, own, came3, came0, side, cuts=peers))
    else:
        parts = lax.all_to_all(parts[0], "seq", 0, 0, tiled=True)
        chosen = (jnp.arange(units)[:, None] == wanted[None, :]) & (used[None, :] > 0)
        total = jnp.dot(
            chosen.astype(jnp.bfloat16),
            parts.reshape(parts.shape[0], -1),
            preferred_element_type=jnp.float32,
        )
        dq = exchange(dq)
        dkv = exchange(add_rounded(units, own, total.reshape(own.shape), cuts=peers))
    return unpack(me_ref, dq, dkv)


def solution(mesh):
    rows = P(("seq", "head"), None)
    in_specs = (rows, rows, rows, rows, rows, P("seq", "head"), P(None, "head", None))
    return jax.shard_map(
        body, mesh=mesh, in_specs=in_specs, out_specs=(rows, rows, rows), check_vma=False
    )
```

```python
import functools

import jax
import jax.numpy as jnp
from jax import lax
from jax.experimental import pallas as pl
from jax.experimental.pallas import tpu as pltpu
from jax.sharding import PartitionSpec as P

HD = 128
QB = 128
KB = 64
NSEL = 4
GROUP = 4
SCALE = HD ** (-0.5)
STAT = 16

VMEM = pl.BlockSpec(memory_space=pltpu.VMEM)
ANY = pl.BlockSpec(memory_space=pl.ANY)
HBM = pl.BlockSpec(memory_space=pltpu.HBM)
SMEM = pl.BlockSpec(memory_space=pltpu.SMEM)
NT = (((1,), (1,)), ((), ()))
TN = (((0,), (0,)), ((), ()))
PACK_PARAMS = pltpu.CompilerParams(vmem_limit_bytes=60 * 1024 * 1024)
PARAMS = pltpu.CompilerParams(vmem_limit_bytes=24 * 1024 * 1024)


def dot(a, b, dims=(((1,), (0,)), ((), ()))):
    return lax.dot_general(a, b, dims, preferred_element_type=jnp.float32)


def lanes(index, width):
    return pl.ds(pl.multiple_of(index * width, width), width)


def run_copies(pairs, sems):
    copies = [
        pltpu.make_async_copy(source, target, sems.at[i])
        for i, (source, target) in enumerate(pairs)
    ]
    for copy in copies:
        copy.start()
    return copies


def pack_kv_kernel(peers, me_ref, k_ref, v_ref, *refs):
    out_refs, sems = refs[:peers], refs[peers]
    kv_heads = out_refs[0].shape[0]
    pairs = []
    for c, out_ref in reversed(list(enumerate(out_refs))):
        for g in range(kv_heads):
            cols = lanes((me_ref[0] ^ c) * kv_heads + g, HD)
            pairs.append((k_ref.at[:, cols], out_ref.at[g, :, pl.ds(0, HD)]))
            pairs.append((v_ref.at[:, cols], out_ref.at[g, :, pl.ds(HD, HD)]))
    for copy in run_copies(pairs, sems):
        copy.wait()


def pack_kv(me, keys, values, peers):
    tokens, width = keys.shape
    kv_heads = width // HD // peers
    piece = jax.ShapeDtypeStruct((kv_heads, tokens, 2 * HD), jnp.bfloat16)
    return pl.pallas_call(
        functools.partial(pack_kv_kernel, peers),
        out_shape=(piece,) * peers,
        in_specs=[SMEM, HBM, HBM],
        out_specs=(VMEM,) * peers,
        scratch_shapes=[pltpu.SemaphoreType.DMA((2 * peers * kv_heads,))],
        compiler_params=PACK_PARAMS,
    )(me, keys, values)


def three_pieces(x):
    hi = x.astype(jnp.bfloat16)
    rest = x - hi.astype(jnp.float32)
    mid = rest.astype(jnp.bfloat16)
    low = (rest - mid.astype(jnp.float32)).astype(jnp.bfloat16)
    return hi, mid, low


def pack_q_kernel(peers, me_ref, q_any, do_any, o_any, *refs):
    half = peers // 2
    rows = refs[0].shape[0]
    out_refs = refs[:half] + tuple(refs[half].at[i * rows : (i + 1) * rows] for i in range(half))
    q_ref, do_ref, o_ref, sems = refs[half + 1 :]
    for copy in run_copies([(q_any, q_ref), (do_any, do_ref), (o_any, o_ref)], sems):
        copy.wait()
    heads = (out_refs[0].shape[0] - STAT) // KB
    lane = lax.broadcasted_iota(jnp.int32, (KB, HD), 1)
    delta = jnp.zeros((KB, HD), jnp.float32)
    for c, out_ref in enumerate(out_refs):
        for h in range(heads):
            cols = lanes((me_ref[0] ^ c) * heads + h, HD)
            do = do_ref[:, cols]
            out_ref[h * KB : (h + 1) * KB, :HD] = q_ref[:, cols]
            out_ref[h * KB : (h + 1) * KB, HD:] = do
            products = do.astype(jnp.float32) * o_ref[:, cols].astype(jnp.float32)
            total = jnp.sum(products, axis=-1, keepdims=True)
            delta = jnp.where(lane == c * heads + h, total, delta)
    by_head = delta.T
    for c, out_ref in enumerate(out_refs):
        hi, mid, low = three_pieces(by_head[c * heads : (c + 1) * heads])
        base = heads * KB
        zero = jnp.zeros((heads, HD - KB), jnp.bfloat16)
        first = jnp.concatenate([hi, zero, mid, zero], axis=1)
        second = jnp.concatenate([low, zero, zero, jnp.zeros_like(low)], axis=1)
        out_ref[base : base + STAT, :] = jnp.concatenate([first, second], axis=0)


def pack_q(me, queries, grad_out, outputs_saved, peers):
    tokens, width = queries.shape
    heads = width // HD // peers
    half = peers // 2
    rows = heads * tokens + STAT
    piece = jax.ShapeDtypeStruct((rows, 2 * HD), jnp.bfloat16)
    far = jax.ShapeDtypeStruct((half * rows, 2 * HD), jnp.bfloat16)
    return pl.pallas_call(
        functools.partial(pack_q_kernel, peers),
        out_shape=(piece,) * half + (far,),
        in_specs=[SMEM] + [HBM] * 3,
        out_specs=(VMEM,) * (half + 1),
        scratch_shapes=[pltpu.VMEM(queries.shape, jnp.bfloat16)] * 3
        + [pltpu.SemaphoreType.DMA((3,))],
        compiler_params=PACK_PARAMS,
    )(me, queries, grad_out, outputs_saved)


def query_rows(qdo, c, h):
    rows = slice(h * KB, (h + 1) * KB)
    pair = (qdo[c], qdo[c ^ 1])
    q = jnp.concatenate([ref[rows, :HD] for ref in pair], axis=0)
    do = jnp.concatenate([ref[rows, HD:] for ref in pair], axis=0)
    return q, do


def own_kernel(peers, me_ref, own_kv_ref, stats_ref, *refs):
    qdo = refs[:peers]
    listed_refs = refs[peers : 2 * peers]
    half = peers // 2
    *dq_refs, far_ref, own_ref = refs[2 * peers :]
    dq_refs += [far_ref.at[i * KB : (i + 1) * KB] for i in range(half)]
    heads = (qdo[0].shape[0] - STAT) // KB
    kv_heads = heads // GROUP
    key_row = lax.broadcasted_iota(jnp.int32, (QB, QB), 0)
    query_row = lax.broadcasted_iota(jnp.int32, (QB, QB), 1)
    swapped = jnp.where((me_ref[0] & 1) == 1, KB, 0)
    causal = (key_row ^ swapped) <= (query_row ^ swapped)
    for c in range(0, peers, 2):
        for g in range(kv_heads):
            own = [(c + i) * kv_heads + g for i in range(2)]
            kv = jnp.concatenate([own_kv_ref[u] for u in own], axis=0)
            k = kv[:, :HD]
            v = kv[:, HD:]
            dk = jnp.zeros((QB, HD), jnp.float32)
            dv = jnp.zeros((QB, HD), jnp.float32)
            for h in range(g * GROUP, (g + 1) * GROUP):
                q, do = query_rows(qdo, c, h)
                lse_row = stats_ref[0, h : h + 1, c * KB : c * KB + QB]
                delta_row = stats_ref[1, h : h + 1, c * KB : c * KB + QB]
                prob = jnp.where(causal, jnp.exp(dot(k, q, NT) * SCALE - lse_row), 0.0)
                score = (prob * (dot(v, do, NT) - delta_row)).astype(jnp.bfloat16)
                dq = dot(score, k, TN) * SCALE
                cols = slice(h * HD, (h + 1) * HD)
                for i in range(2):
                    part = listed_refs[c + i][:, cols] + dq[i * KB : (i + 1) * KB]
                    dq_refs[c + i][:, cols] = part.astype(jnp.bfloat16)
                dk += dot(score, q)
                dv += dot(prob.astype(jnp.bfloat16), do)
            for i in range(2):
                own_ref[own[i], :, :HD] = dk[i * KB : (i + 1) * KB] * SCALE
                own_ref[own[i], :, HD:] = dv[i * KB : (i + 1) * KB]


def own_terms(me, own_kv, stats, qdo, listed):
    peers = len(qdo)
    half = peers // 2
    rows, width = listed[0].shape
    piece = jax.ShapeDtypeStruct((rows, width), jnp.bfloat16)
    far = jax.ShapeDtypeStruct((half * rows, width), jnp.bfloat16)
    outs = pl.pallas_call(
        functools.partial(own_kernel, peers),
        out_shape=(piece,) * half + (far, jax.ShapeDtypeStruct(own_kv.shape, jnp.float32)),
        in_specs=[SMEM] + [VMEM] * (2 + 2 * peers),
        out_specs=(VMEM,) * (half + 2),
        compiler_params=PARAMS,
        cost_estimate=pl.CostEstimate(
            flops=335_000_000, bytes_accessed=4_000_000, transcendentals=260_000
        ),
    )(me, own_kv, stats, *qdo, *listed)
    return list(outs[:-1]), outs[-1]


def row_stats(me, qdo, lse_ref, stats_ref):
    peers = len(qdo)
    heads = (qdo[0].shape[0] - STAT) // KB
    base = heads * KB
    lse_blocks = [lse_ref[:, c * KB : (c + 1) * KB] for c in range(peers)]
    for c in range(peers):
        first = qdo[c][base : base + heads, :].astype(jnp.float32)
        second = qdo[c][base + heads : base + 2 * heads, :].astype(jnp.float32)
        delta = first[:, :KB] + first[:, HD : HD + KB] + second[:, :KB]
        lse_here = lse_blocks[0]
        for t in range(1, peers):
            lse_here = jnp.where((me ^ c) == t, lse_blocks[t], lse_here)
        stats_ref[0, :, c * KB : (c + 1) * KB] = lse_here
        stats_ref[1, :, c * KB : (c + 1) * KB] = delta


def listed_kernel(peers, me_ref, slot_ref, lse_ref, kv, *refs):
    qdo, outs, sums = refs[:peers], refs[peers:-1], refs[-1]
    stats_ref, dq_refs, part_refs = outs[0], outs[1 : peers + 1], outs[peers + 1 :]
    row_stats(me_ref[0], qdo, lse_ref, stats_ref)
    heads = (qdo[0].shape[0] - STAT) // KB
    sums[...] = jnp.zeros_like(sums)

    def scores(c, h):
        q, do = query_rows(qdo, c, h)
        slots = [slot_ref[(c // 2 * heads + h) * NSEL + n] for n in range(NSEL)]
        rows_kv = jnp.concatenate([kv[s] for s in slots], axis=0)
        k = rows_kv[:, :HD]
        v = rows_kv[:, HD:]
        lse_row = stats_ref[0, h : h + 1, c * KB : c * KB + QB]
        delta_row = stats_ref[1, h : h + 1, c * KB : c * KB + QB]
        prob = jnp.exp(dot(k, q, NT) * SCALE - lse_row)
        score = (prob * (dot(v, do, NT) - delta_row)).astype(jnp.bfloat16)
        return c, h, slots, q, do, k, prob.astype(jnp.bfloat16), score

    def gradients(c, h, slots, q, do, k, prob, score):
        dq = dot(score, k, TN) * SCALE
        cols = slice(h * HD, (h + 1) * HD)
        for i in range(2):
            dq_refs[c + i][:, cols] = dq[i * KB : (i + 1) * KB]
        dk = dot(score, q) * SCALE
        dv = dot(prob, do)
        for n in range(NSEL):
            part = slice(n * KB, (n + 1) * KB)
            sums[slots[n], :, :HD] += dk[part]
            sums[slots[n], :, HD:] += dv[part]

    waiting = []
    for c in range(0, peers, 2):
        for h in range(heads):
            waiting.append(scores(c, h))
            if len(waiting) > 2:
                gradients(*waiting.pop(0))
    for state in waiting:
        gradients(*state)
    first = 0
    for part_ref in part_refs:
        part_ref[...] = sums[first : first + part_ref.shape[0]].astype(part_ref.dtype)
        first += part_ref.shape[0]


def listed_terms(me, slots, lse, kv, qdo, parts):
    peers = len(qdo)
    heads, tokens = lse.shape
    outs = pl.pallas_call(
        functools.partial(listed_kernel, peers),
        out_shape=(
            jax.ShapeDtypeStruct((2, heads, tokens), jnp.float32),
            *[jax.ShapeDtypeStruct((KB, heads * HD), jnp.float32)] * peers,
            *[jax.ShapeDtypeStruct((units,) + kv.shape[1:], kind) for units, kind in parts],
        ),
        in_specs=[SMEM, SMEM] + [VMEM] * (2 + peers),
        out_specs=(VMEM,) * (1 + peers + len(parts)),
        scratch_shapes=[pltpu.VMEM(kv.shape, jnp.float32)],
        compiler_params=PARAMS,
        cost_estimate=pl.CostEstimate(
            flops=671_000_000, bytes_accessed=8_000_000, transcendentals=530_000
        ),
    )(me, slots, lse, kv, *qdo)
    return outs[0], outs[1 : peers + 1], outs[peers + 1 :]


def add_kernel(firsts, *refs):
    terms, out_refs = refs[: len(firsts)], refs[len(firsts) :]
    done = 0
    for out_ref in out_refs:
        size = out_ref.shape[0]
        total = None
        for ref, first in zip(terms, firsts):
            part = ref[first + done : first + done + size].astype(jnp.float32)
            total = part if total is None else total + part
        out_ref[...] = total.astype(out_ref.dtype)
        done += size


def add_rounded(units, *terms, cuts=1, kind=jnp.bfloat16, bytes_moved=2_000_000):
    terms = [term if isinstance(term, tuple) else (term, 0) for term in terms]
    arrays = [array for array, _ in terms]
    piece = jax.ShapeDtypeStruct((units // cuts,) + arrays[0].shape[1:], kind)
    outs = pl.pallas_call(
        functools.partial(add_kernel, [first for _, first in terms]),
        out_shape=(piece,) * cuts,
        in_specs=[VMEM] * len(arrays),
        out_specs=(VMEM,) * cuts,
        compiler_params=PARAMS,
        cost_estimate=pl.CostEstimate(
            flops=2_000_000, bytes_accessed=bytes_moved, transcendentals=0
        ),
    )(*arrays)
    return outs if cuts > 1 else outs[0]


def unpack_q_kernel(peers, me_ref, *refs):
    gq_ref = refs[peers]
    width = refs[0].shape[1]
    for c in range(peers):
        gq_ref[:, lanes(me_ref[0] ^ c, width)] = refs[c][...]


def unpack_kv_kernel(peers, me_ref, *refs):
    gk_ref, gv_ref = refs[peers:]
    kv_heads = refs[0].shape[0]
    for c in range(peers):
        for g in range(kv_heads):
            cols = lanes((me_ref[0] ^ c) * kv_heads + g, HD)
            gk_ref[:, cols] = refs[c][g, :, :HD]
            gv_ref[:, cols] = refs[c][g, :, HD:]


def unpack(me, dq, dkv):
    peers = len(dq)
    tokens, width = dq[0].shape
    kv_width = dkv[0].shape[0] * peers * HD
    spec = [SMEM] + [VMEM] * peers
    grad_q = pl.pallas_call(
        functools.partial(unpack_q_kernel, peers),
        out_shape=jax.ShapeDtypeStruct((tokens, peers * width), jnp.bfloat16),
        in_specs=spec,
        out_specs=VMEM,
        compiler_params=PARAMS,
    )(me, *dq)
    grad_q, dkv[0] = lax.optimization_barrier((grad_q, dkv[0]))
    grad_k, grad_v = pl.pallas_call(
        functools.partial(unpack_kv_kernel, peers),
        out_shape=(jax.ShapeDtypeStruct((tokens, kv_width), jnp.bfloat16),) * 2,
        in_specs=spec,
        out_specs=(VMEM, VMEM),
        compiler_params=PARAMS,
    )(me, *dkv)
    return grad_q, grad_k, grad_v


def exchange(pieces):
    peers = len(pieces)
    moved = [
        lax.ppermute(pieces[c], "head", [(h, h ^ c) for h in range(peers)])
        for c in range(1, peers)
    ]
    return [pieces[0]] + moved


def exchange_rows(here, near, far):
    rows = here.shape[0]
    flip = [(h, h ^ 1) for h in range(4)]
    across = [(h, h ^ 2) for h in range(4)]
    far = lax.ppermute(far, "head", across)
    near = lax.ppermute(near, "head", flip)
    return [here, near, far[:rows], lax.ppermute(far[rows:], "head", flip)]


def body(queries, keys, values, outputs_saved, grad_out, lse, block_lists):
    peers = lax.axis_size("head")
    shards = lax.axis_size("seq")
    me = lax.axis_index("seq")
    head_me = lax.axis_index("head")
    me_ref = head_me.astype(jnp.int32).reshape(1)
    heads = lse.shape[1]
    kv_heads = heads // GROUP
    key_count = peers
    units = key_count * kv_heads

    kv_pack = pack_kv(me_ref, keys, values, peers)
    own_kv = jnp.concatenate(exchange(kv_pack), axis=0)

    per_peer = block_lists.reshape(shards, -1)
    requests = per_peer.shape[1]
    order = jnp.arange(requests, dtype=jnp.int32)
    group_of = order % (heads * NSEL) // (NSEL * GROUP)
    block_turn = jnp.where(head_me >= peers // 2, requests // 2, 0)
    capacity = -(-requests // (shards - 1))
    dense = units <= capacity and shards == 8

    if dense:
        far = shards // 2
        swap = [(s, s ^ 1) for s in range(shards)]
        ahead = [(s, (s + 2) % shards) for s in range(shards)]
        back = [(s, (s - 2) % shards) for s in range(shards)]
        same1 = lax.ppermute(own_kv, "seq", ahead)
        cross0 = lax.ppermute(own_kv, "seq", swap)
        later_me, held = lax.optimization_barrier((me_ref, own_kv))
        q_pieces = pack_q(later_me, queries, grad_out, outputs_saved, peers)
        held, q_pieces = lax.optimization_barrier((held, q_pieces))
        same3 = lax.ppermute(held, "seq", back)
        qdo = exchange_rows(*q_pieces)
        per_peer, same1 = lax.optimization_barrier((per_peer, same1))
        mine = lax.dynamic_index_in_dim(per_peer, me, 0, keepdims=False)
        owner = mine // key_count
        apart = (me // 2 - owner // 2) % far
        crossed = (me ^ owner) & 1
        piece = jnp.where(crossed == 1, far - 1 + (apart + 1) % far, apart - 1)
        slots = piece * units + (mine % key_count ^ head_me) * kv_heads + group_of
        slots = jnp.roll(slots, block_turn)
        same2 = lax.ppermute(same1, "seq", ahead)
        cross1 = lax.ppermute(same1, "seq", swap)
        cross3 = lax.ppermute(same3, "seq", swap)
        held, cross1 = lax.optimization_barrier((same2, cross1))
        cross2 = lax.ppermute(held, "seq", swap)
        kv_all = jnp.zeros((7 * units,) + own_kv.shape[1:], jnp.bfloat16)
        arriving = [(same1, 0), (cross0, 4), (cross1, 5), (same2, 1), (same3, 2)]
        for array, at in arriving + [(cross2, 6), (cross3, 3)]:
            kv_all = lax.dynamic_update_slice_in_dim(kv_all, array, at * units, 0)
        wide, low = jnp.float32, jnp.bfloat16
        part_types = [(1, wide), (1, wide), (2, low), (1, wide), (1, low), (1, low)]
        part_types = [(count * units, kind) for count, kind in part_types]
    else:
        owner = per_peer // key_count
        earlier = (owner[:, :, None] == owner[:, None, :]) & (order[None, :] < order[:, None])
        position = jnp.sum(earlier.astype(jnp.int32), axis=2)
        slots = lax.dynamic_index_in_dim(owner * capacity + position, me, 0, keepdims=False)
        hits = (owner == me)[:, :, None] & (position[:, :, None] == jnp.arange(capacity))
        hits = hits.astype(jnp.int32)
        used = jnp.sum(hits, axis=1).reshape(-1)
        wanted = (per_peer % key_count ^ head_me) * kv_heads + group_of[None, :]
        wanted = jnp.sum(hits * wanted[:, :, None], axis=1).reshape(-1)
        kv_all = lax.all_to_all(own_kv[wanted], "seq", 0, 0, tiled=True)
        part_types = [(kv_all.shape[0], jnp.bfloat16)]
        slots = jnp.roll(slots, block_turn)
        qdo = exchange_rows(*pack_q(me_ref, queries, grad_out, outputs_saved, peers))

    stats, listed, parts = listed_terms(me_ref, slots, lse.T, kv_all, qdo, part_types)
    dq, own = own_terms(me_ref, own_kv, stats, qdo, listed)

    if dense:
        stay1, stay2, away3, leave0, leave1, leave2 = parts
        came2 = lax.ppermute(leave2, "seq", swap)
        came3 = lax.ppermute(away3, "seq", ahead)
        came1 = lax.ppermute(leave1, "seq", swap)
        came2, dq = lax.optimization_barrier((came2, dq))
        hop = lax.ppermute(add_rounded(units, stay2, came2), "seq", back)
        near = add_rounded(units, leave0, (came3, units))
        near, dq = lax.optimization_barrier((near, dq))
        came0 = lax.ppermute(near, "seq", swap)
        base = add_rounded(units, own, came3, came0, kind=jnp.float32, bytes_moved=16_000_000)
        hop, dq[1:2] = lax.optimization_barrier((hop, dq[1:2]))
        side = lax.ppermute(add_rounded(units, stay1, came1, hop), "seq", back)
        dq = exchange_rows(*dq)
        dkv = exchange(add_rounded(units, base, side, cuts=peers))
    else:
        parts = lax.all_to_all(parts[0], "seq", 0, 0, tiled=True)
        chosen = (jnp.arange(units)[:, None] == wanted[None, :]) & (used[None, :] > 0)
        total = jnp.dot(
            chosen.astype(jnp.bfloat16),
            parts.reshape(parts.shape[0], -1),
            preferred_element_type=jnp.float32,
        )
        dq = exchange_rows(*dq)
        dkv = exchange(add_rounded(units, own, total.reshape(own.shape), cuts=peers))
    return unpack(me_ref, dq, dkv)


def solution(mesh):
    rows = P(("seq", "head"), None)
    in_specs = (rows, rows, rows, rows, rows, P("seq", "head"), P(None, "head", None))
    return jax.shard_map(
        body, mesh=mesh, in_specs=in_specs, out_specs=(rows, rows, rows), check_vma=False
    )
```

```python
import functools

import jax
import jax.numpy as jnp
from jax import lax
from jax.experimental import pallas as pl
from jax.experimental.pallas import tpu as pltpu
from jax.sharding import PartitionSpec as P

HD = 128
QB = 128
KB = 64
NSEL = 4
GROUP = 4
SCALE = HD ** (-0.5)
STAT = 16

VMEM = pl.BlockSpec(memory_space=pltpu.VMEM)
ANY = pl.BlockSpec(memory_space=pl.ANY)
HBM = pl.BlockSpec(memory_space=pltpu.HBM)
SMEM = pl.BlockSpec(memory_space=pltpu.SMEM)
NT = (((1,), (1,)), ((), ()))
TN = (((0,), (0,)), ((), ()))
PACK_PARAMS = pltpu.CompilerParams(vmem_limit_bytes=60 * 1024 * 1024)
PARAMS = pltpu.CompilerParams(vmem_limit_bytes=24 * 1024 * 1024)


def dot(a, b, dims=(((1,), (0,)), ((), ()))):
    return lax.dot_general(a, b, dims, preferred_element_type=jnp.float32)


def lanes(index, width):
    return pl.ds(pl.multiple_of(index * width, width), width)


def run_copies(pairs, sems):
    copies = [
        pltpu.make_async_copy(source, target, sems.at[i])
        for i, (source, target) in enumerate(pairs)
    ]
    for copy in copies:
        copy.start()
    return copies


def pack_kv_kernel(peers, me_ref, k_ref, v_ref, *refs):
    out_refs, sems = refs[:peers], refs[peers]
    kv_heads = out_refs[0].shape[0]
    pairs = []
    for c, out_ref in reversed(list(enumerate(out_refs))):
        for g in range(kv_heads):
            cols = lanes((me_ref[0] ^ c) * kv_heads + g, HD)
            pairs.append((k_ref.at[:, cols], out_ref.at[g, :, pl.ds(0, HD)]))
            pairs.append((v_ref.at[:, cols], out_ref.at[g, :, pl.ds(HD, HD)]))
    for copy in run_copies(pairs, sems):
        copy.wait()


def pack_kv(me, keys, values, peers):
    tokens, width = keys.shape
    kv_heads = width // HD // peers
    piece = jax.ShapeDtypeStruct((kv_heads, tokens, 2 * HD), jnp.bfloat16)
    return pl.pallas_call(
        functools.partial(pack_kv_kernel, peers),
        out_shape=(piece,) * peers,
        in_specs=[SMEM, HBM, HBM],
        out_specs=(VMEM,) * peers,
        scratch_shapes=[pltpu.SemaphoreType.DMA((2 * peers * kv_heads,))],
        compiler_params=PACK_PARAMS,
    )(me, keys, values)


def three_pieces(x):
    hi = x.astype(jnp.bfloat16)
    rest = x - hi.astype(jnp.float32)
    mid = rest.astype(jnp.bfloat16)
    low = (rest - mid.astype(jnp.float32)).astype(jnp.bfloat16)
    return hi, mid, low


def pack_q_kernel(peers, me_ref, q_any, do_any, o_any, *refs):
    half = peers // 2
    rows = refs[0].shape[0]
    out_refs = refs[:half] + tuple(refs[half].at[i * rows : (i + 1) * rows] for i in range(half))
    q_ref, do_ref, o_ref, sems = refs[half + 1 :]
    for copy in run_copies([(q_any, q_ref), (do_any, do_ref), (o_any, o_ref)], sems):
        copy.wait()
    heads = (out_refs[0].shape[0] - STAT) // KB
    lane = lax.broadcasted_iota(jnp.int32, (KB, HD), 1)
    delta = jnp.zeros((KB, HD), jnp.float32)
    for c, out_ref in enumerate(out_refs):
        for h in range(heads):
            cols = lanes((me_ref[0] ^ c) * heads + h, HD)
            do = do_ref[:, cols]
            out_ref[h * KB : (h + 1) * KB, :HD] = q_ref[:, cols]
            out_ref[h * KB : (h + 1) * KB, HD:] = do
            products = do.astype(jnp.float32) * o_ref[:, cols].astype(jnp.float32)
            total = jnp.sum(products, axis=-1, keepdims=True)
            delta = jnp.where(lane == c * heads + h, total, delta)
    by_head = delta.T
    for c, out_ref in enumerate(out_refs):
        hi, mid, low = three_pieces(by_head[c * heads : (c + 1) * heads])
        base = heads * KB
        zero = jnp.zeros((heads, HD - KB), jnp.bfloat16)
        first = jnp.concatenate([hi, zero, mid, zero], axis=1)
        second = jnp.concatenate([low, zero, zero, jnp.zeros_like(low)], axis=1)
        out_ref[base : base + STAT, :] = jnp.concatenate([first, second], axis=0)


def pack_q(me, queries, grad_out, outputs_saved, peers):
    tokens, width = queries.shape
    heads = width // HD // peers
    half = peers // 2
    rows = heads * tokens + STAT
    piece = jax.ShapeDtypeStruct((rows, 2 * HD), jnp.bfloat16)
    far = jax.ShapeDtypeStruct((half * rows, 2 * HD), jnp.bfloat16)
    return pl.pallas_call(
        functools.partial(pack_q_kernel, peers),
        out_shape=(piece,) * half + (far,),
        in_specs=[SMEM] + [HBM] * 3,
        out_specs=(VMEM,) * (half + 1),
        scratch_shapes=[pltpu.VMEM(queries.shape, jnp.bfloat16)] * 3
        + [pltpu.SemaphoreType.DMA((3,))],
        compiler_params=PACK_PARAMS,
    )(me, queries, grad_out, outputs_saved)


def query_rows(qdo, c, h):
    rows = slice(h * KB, (h + 1) * KB)
    pair = (qdo[c], qdo[c ^ 1])
    q = jnp.concatenate([ref[rows, :HD] for ref in pair], axis=0)
    do = jnp.concatenate([ref[rows, HD:] for ref in pair], axis=0)
    return q, do


def own_kernel(peers, me_ref, own_kv_ref, stats_ref, *refs):
    qdo = refs[:peers]
    listed_refs = refs[peers : 2 * peers]
    half = peers // 2
    *dq_refs, far_ref, own_ref = refs[2 * peers :]
    dq_refs += [far_ref.at[i * KB : (i + 1) * KB] for i in range(half)]
    heads = (qdo[0].shape[0] - STAT) // KB
    kv_heads = heads // GROUP
    key_row = lax.broadcasted_iota(jnp.int32, (QB, QB), 0)
    query_row = lax.broadcasted_iota(jnp.int32, (QB, QB), 1)
    swapped = jnp.where((me_ref[0] & 1) == 1, KB, 0)
    causal = (key_row ^ swapped) <= (query_row ^ swapped)
    for c in range(0, peers, 2):
        for g in range(kv_heads):
            own = [(c + i) * kv_heads + g for i in range(2)]
            kv = jnp.concatenate([own_kv_ref[u] for u in own], axis=0)
            k = kv[:, :HD]
            v = kv[:, HD:]
            dk = jnp.zeros((QB, HD), jnp.float32)
            dv = jnp.zeros((QB, HD), jnp.float32)
            for h in range(g * GROUP, (g + 1) * GROUP):
                q, do = query_rows(qdo, c, h)
                lse_row = stats_ref[0, h : h + 1, c * KB : c * KB + QB]
                delta_row = stats_ref[1, h : h + 1, c * KB : c * KB + QB]
                prob = jnp.where(causal, jnp.exp(dot(k, q, NT) * SCALE - lse_row), 0.0)
                score = (prob * (dot(v, do, NT) - delta_row)).astype(jnp.bfloat16)
                dq = dot(score, k, TN) * SCALE
                cols = slice(h * HD, (h + 1) * HD)
                for i in range(2):
                    part = listed_refs[c + i][:, cols] + dq[i * KB : (i + 1) * KB]
                    dq_refs[c + i][:, cols] = part.astype(jnp.bfloat16)
                dk += dot(score, q)
                dv += dot(prob.astype(jnp.bfloat16), do)
            for i in range(2):
                own_ref[own[i], :, :HD] = dk[i * KB : (i + 1) * KB] * SCALE
                own_ref[own[i], :, HD:] = dv[i * KB : (i + 1) * KB]


def own_terms(me, own_kv, stats, qdo, listed):
    peers = len(qdo)
    half = peers // 2
    rows, width = listed[0].shape
    piece = jax.ShapeDtypeStruct((rows, width), jnp.bfloat16)
    far = jax.ShapeDtypeStruct((half * rows, width), jnp.bfloat16)
    outs = pl.pallas_call(
        functools.partial(own_kernel, peers),
        out_shape=(piece,) * half + (far, jax.ShapeDtypeStruct(own_kv.shape, jnp.float32)),
        in_specs=[SMEM] + [VMEM] * (2 + 2 * peers),
        out_specs=(VMEM,) * (half + 2),
        compiler_params=PARAMS,
        cost_estimate=pl.CostEstimate(
            flops=335_000_000, bytes_accessed=4_000_000, transcendentals=260_000
        ),
    )(me, own_kv, stats, *qdo, *listed)
    return list(outs[:-1]), outs[-1]


def row_stats(me, qdo, lse_ref, stats_ref):
    peers = len(qdo)
    heads = (qdo[0].shape[0] - STAT) // KB
    base = heads * KB
    lse_blocks = [lse_ref[:, c * KB : (c + 1) * KB] for c in range(peers)]
    for c in range(peers):
        first = qdo[c][base : base + heads, :].astype(jnp.float32)
        second = qdo[c][base + heads : base + 2 * heads, :].astype(jnp.float32)
        delta = first[:, :KB] + first[:, HD : HD + KB] + second[:, :KB]
        lse_here = lse_blocks[0]
        for t in range(1, peers):
            lse_here = jnp.where((me ^ c) == t, lse_blocks[t], lse_here)
        stats_ref[0, :, c * KB : (c + 1) * KB] = lse_here
        stats_ref[1, :, c * KB : (c + 1) * KB] = delta


def listed_kernel(peers, me_ref, slot_ref, lse_ref, kv, *refs):
    qdo, outs, sums = refs[:peers], refs[peers:-1], refs[-1]
    stats_ref, dq_refs, part_refs = outs[0], outs[1 : peers + 1], outs[peers + 1 :]
    row_stats(me_ref[0], qdo, lse_ref, stats_ref)
    heads = (qdo[0].shape[0] - STAT) // KB
    sums[...] = jnp.zeros_like(sums)

    def scores(c, h):
        q, do = query_rows(qdo, c, h)
        slots = [slot_ref[(c // 2 * heads + h) * NSEL + n] for n in range(NSEL)]
        rows_kv = jnp.concatenate([kv[s] for s in slots], axis=0)
        k = rows_kv[:, :HD]
        v = rows_kv[:, HD:]
        lse_row = stats_ref[0, h : h + 1, c * KB : c * KB + QB]
        delta_row = stats_ref[1, h : h + 1, c * KB : c * KB + QB]
        prob = jnp.exp(dot(k, q, NT) * SCALE - lse_row)
        score = (prob * (dot(v, do, NT) - delta_row)).astype(jnp.bfloat16)
        return c, h, slots, q, do, k, prob.astype(jnp.bfloat16), score

    def gradients(c, h, slots, q, do, k, prob, score):
        dq = dot(score, k, TN) * SCALE
        cols = slice(h * HD, (h + 1) * HD)
        for i in range(2):
            dq_refs[c + i][:, cols] = dq[i * KB : (i + 1) * KB]
        dk = dot(score, q) * SCALE
        dv = dot(prob, do)
        for n in range(NSEL):
            part = slice(n * KB, (n + 1) * KB)
            sums[slots[n], :, :HD] += dk[part]
            sums[slots[n], :, HD:] += dv[part]

    waiting = []
    for c in range(0, peers, 2):
        for h in range(heads):
            waiting.append(scores(c, h))
            if len(waiting) > 2:
                gradients(*waiting.pop(0))
    for state in waiting:
        gradients(*state)
    first = 0
    for part_ref in part_refs:
        part_ref[...] = sums[first : first + part_ref.shape[0]].astype(part_ref.dtype)
        first += part_ref.shape[0]


def listed_terms(me, slots, lse, kv, qdo, parts):
    peers = len(qdo)
    heads, tokens = lse.shape
    outs = pl.pallas_call(
        functools.partial(listed_kernel, peers),
        out_shape=(
            jax.ShapeDtypeStruct((2, heads, tokens), jnp.float32),
            *[jax.ShapeDtypeStruct((KB, heads * HD), jnp.float32)] * peers,
            *[jax.ShapeDtypeStruct((units,) + kv.shape[1:], kind) for units, kind in parts],
        ),
        in_specs=[SMEM, SMEM] + [VMEM] * (2 + peers),
        out_specs=(VMEM,) * (1 + peers + len(parts)),
        scratch_shapes=[pltpu.VMEM(kv.shape, jnp.float32)],
        compiler_params=PARAMS,
        cost_estimate=pl.CostEstimate(
            flops=671_000_000, bytes_accessed=8_000_000, transcendentals=530_000
        ),
    )(me, slots, lse, kv, *qdo)
    return outs[0], outs[1 : peers + 1], outs[peers + 1 :]


def add_kernel(firsts, *refs):
    terms, out_refs = refs[: len(firsts)], refs[len(firsts) :]
    done = 0
    for out_ref in out_refs:
        size = out_ref.shape[0]
        total = None
        for ref, first in zip(terms, firsts):
            part = ref[first + done : first + done + size].astype(jnp.float32)
            total = part if total is None else total + part
        out_ref[...] = total.astype(out_ref.dtype)
        done += size


def add_parts(outs, *terms, bytes_moved=2_000_000):
    terms = [term if isinstance(term, tuple) else (term, 0) for term in terms]
    arrays = [array for array, _ in terms]
    tail = arrays[0].shape[1:]
    return pl.pallas_call(
        functools.partial(add_kernel, [first for _, first in terms]),
        out_shape=[jax.ShapeDtypeStruct((size,) + tail, kind) for size, kind in outs],
        in_specs=[VMEM] * len(arrays),
        out_specs=[VMEM] * len(outs),
        compiler_params=PARAMS,
        cost_estimate=pl.CostEstimate(
            flops=2_000_000, bytes_accessed=bytes_moved, transcendentals=0
        ),
    )(*arrays)


def add_rounded(units, *terms):
    return add_parts([(units, jnp.bfloat16)], *terms)[0]


def unpack_q_kernel(peers, me_ref, *refs):
    gq_ref = refs[peers]
    width = refs[0].shape[1]
    for c in range(peers):
        gq_ref[:, lanes(me_ref[0] ^ c, width)] = refs[c][...]


def unpack_kv_kernel(counts, me_ref, *refs):
    *term_refs, gk_ref, gv_ref = refs
    kv_heads = refs[0].shape[0]
    at = 0
    for c, count in enumerate(counts):
        terms = term_refs[at : at + count]
        at += count
        for g in range(kv_heads):
            cols = lanes((me_ref[0] ^ c) * kv_heads + g, HD)
            total = terms[0][g]
            if count > 1:
                total = sum(term[g].astype(jnp.float32) for term in terms).astype(jnp.bfloat16)
            gk_ref[:, cols] = total[:, :HD]
            gv_ref[:, cols] = total[:, HD:]


def unpack(me, dq, dkv):
    peers = len(dq)
    tokens, width = dq[0].shape
    kv_width = dkv[0][0].shape[0] * peers * HD
    grad_q = pl.pallas_call(
        functools.partial(unpack_q_kernel, peers),
        out_shape=jax.ShapeDtypeStruct((tokens, peers * width), jnp.bfloat16),
        in_specs=[SMEM] + [VMEM] * peers,
        out_specs=VMEM,
        compiler_params=PARAMS,
    )(me, *dq)
    flat = [term for terms in dkv for term in terms]
    grad_q, flat[0] = lax.optimization_barrier((grad_q, flat[0]))
    grad_k, grad_v = pl.pallas_call(
        functools.partial(unpack_kv_kernel, [len(terms) for terms in dkv]),
        out_shape=(jax.ShapeDtypeStruct((tokens, kv_width), jnp.bfloat16),) * 2,
        in_specs=[SMEM] + [VMEM] * len(flat),
        out_specs=(VMEM, VMEM),
        compiler_params=PARAMS,
    )(me, *flat)
    return grad_q, grad_k, grad_v


def exchange(pieces):
    peers = len(pieces)
    moved = [
        lax.ppermute(pieces[c], "head", [(h, h ^ c) for h in range(peers)])
        for c in range(1, peers)
    ]
    return [pieces[0]] + moved


def exchange_rows(here, near, far):
    rows = here.shape[0]
    flip = [(h, h ^ 1) for h in range(4)]
    across = [(h, h ^ 2) for h in range(4)]
    far = lax.ppermute(far, "head", across)
    near = lax.ppermute(near, "head", flip)
    return [here, near, far[:rows], lax.ppermute(far[rows:], "head", flip)]


def send_back(piece, c, shards, peers):
    pairs = [
        (s * peers + h, (s - 2) % shards * peers + (h ^ c))
        for s in range(shards)
        for h in range(peers)
    ]
    return lax.ppermute(piece, ("seq", "head"), pairs)


def body(queries, keys, values, outputs_saved, grad_out, lse, block_lists):
    peers = lax.axis_size("head")
    shards = lax.axis_size("seq")
    me = lax.axis_index("seq")
    head_me = lax.axis_index("head")
    me_ref = head_me.astype(jnp.int32).reshape(1)
    heads = lse.shape[1]
    kv_heads = heads // GROUP
    key_count = peers
    units = key_count * kv_heads

    kv_pack = pack_kv(me_ref, keys, values, peers)
    own_kv = jnp.concatenate(exchange(kv_pack), axis=0)

    per_peer = block_lists.reshape(shards, -1)
    requests = per_peer.shape[1]
    order = jnp.arange(requests, dtype=jnp.int32)
    group_of = order % (heads * NSEL) // (NSEL * GROUP)
    block_turn = jnp.where(head_me >= peers // 2, requests // 2, 0)
    capacity = -(-requests // (shards - 1))
    dense = units <= capacity and shards == 8

    if dense:
        far = shards // 2
        swap = [(s, s ^ 1) for s in range(shards)]
        ahead = [(s, (s + 2) % shards) for s in range(shards)]
        back = [(s, (s - 2) % shards) for s in range(shards)]
        same1 = lax.ppermute(own_kv, "seq", ahead)
        cross0 = lax.ppermute(own_kv, "seq", swap)
        later_me, held = lax.optimization_barrier((me_ref, own_kv))
        q_pieces = pack_q(later_me, queries, grad_out, outputs_saved, peers)
        per_peer, q_pieces = lax.optimization_barrier((per_peer, q_pieces))
        qdo = exchange_rows(*q_pieces)
        mine = lax.dynamic_index_in_dim(per_peer, me, 0, keepdims=False)
        owner = mine // key_count
        apart = (me // 2 - owner // 2) % far
        crossed = (me ^ owner) & 1
        piece = jnp.where(crossed == 1, far - 1 + (apart + 1) % far, apart - 1)
        slots = piece * units + (mine % key_count ^ head_me) * kv_heads + group_of
        slots = jnp.roll(slots, block_turn)
        held, slots = lax.optimization_barrier((held, slots))
        same3 = lax.ppermute(held, "seq", back)
        same2 = lax.ppermute(same1, "seq", ahead)
        cross1 = lax.ppermute(same1, "seq", swap)
        cross3 = lax.ppermute(same3, "seq", swap)
        held, cross1 = lax.optimization_barrier((same2, cross1))
        cross2 = lax.ppermute(held, "seq", swap)
        kv_all = jnp.zeros((7 * units,) + own_kv.shape[1:], jnp.bfloat16)
        arriving = [(same1, 0), (cross0, 4), (cross1, 5), (same2, 1), (same3, 2)]
        for array, at in arriving + [(cross2, 6), (cross3, 3)]:
            kv_all = lax.dynamic_update_slice_in_dim(kv_all, array, at * units, 0)
        wide, low = jnp.float32, jnp.bfloat16
        part_types = [(1, wide), (1, wide), (2, low), (1, wide), (1, low), (1, low)]
        part_types = [(count * units, kind) for count, kind in part_types]
    else:
        owner = per_peer // key_count
        earlier = (owner[:, :, None] == owner[:, None, :]) & (order[None, :] < order[:, None])
        position = jnp.sum(earlier.astype(jnp.int32), axis=2)
        slots = lax.dynamic_index_in_dim(owner * capacity + position, me, 0, keepdims=False)
        hits = (owner == me)[:, :, None] & (position[:, :, None] == jnp.arange(capacity))
        hits = hits.astype(jnp.int32)
        used = jnp.sum(hits, axis=1).reshape(-1)
        wanted = (per_peer % key_count ^ head_me) * kv_heads + group_of[None, :]
        wanted = jnp.sum(hits * wanted[:, :, None], axis=1).reshape(-1)
        kv_all = lax.all_to_all(own_kv[wanted], "seq", 0, 0, tiled=True)
        part_types = [(kv_all.shape[0], jnp.bfloat16)]
        slots = jnp.roll(slots, block_turn)
        qdo = exchange_rows(*pack_q(me_ref, queries, grad_out, outputs_saved, peers))

    stats, listed, parts = listed_terms(me_ref, slots, lse.T, kv_all, qdo, part_types)
    dq, own = own_terms(me_ref, own_kv, stats, qdo, listed)

    if dense:
        stay1, stay2, away3, leave0, leave1, leave2 = parts
        came2 = lax.ppermute(leave2, "seq", swap)
        came3 = lax.ppermute(away3, "seq", ahead)
        came1 = lax.ppermute(leave1, "seq", swap)
        came2, dq = lax.optimization_barrier((came2, dq))
        hop = lax.ppermute(add_rounded(units, stay2, came2), "seq", back)
        near = add_rounded(units, leave0, (came3, units))
        near, dq = lax.optimization_barrier((near, dq))
        came0 = lax.ppermute(near, "seq", swap)
        half, pair = units // 2, units // peers
        outs = [(half, wide), (pair, low), (pair, low)]
        base, *base_far = add_parts(outs, own, came3, came0, bytes_moved=16_000_000)
        base, dq[1:2] = lax.optimization_barrier((base, dq[1:2]))
        outs = [(half, low), (pair, low), (pair, low)]
        side, *side_far = add_parts(outs, stay1, came1, hop)
        side_far = [send_back(piece, c, shards, peers) for c, piece in zip((2, 3), side_far)]
        side = lax.ppermute(side, "seq", back)
        dq = exchange_rows(*dq)
        base_far = [
            lax.ppermute(piece, "head", [(h, h ^ c) for h in range(peers)])
            for c, piece in zip((2, 3), base_far)
        ]
        side, base_far, side_far = lax.optimization_barrier((side, base_far, side_far))
        here, near = add_parts([(pair, low)] * 2, base, side)
        near = lax.ppermute(near, "head", [(h, h ^ 1) for h in range(peers)])
        dkv = [[here], [near]] + [list(terms) for terms in zip(base_far, side_far)]
    else:
        parts = lax.all_to_all(parts[0], "seq", 0, 0, tiled=True)
        chosen = (jnp.arange(units)[:, None] == wanted[None, :]) & (used[None, :] > 0)
        total = jnp.dot(
            chosen.astype(jnp.bfloat16),
            parts.reshape(parts.shape[0], -1),
            preferred_element_type=jnp.float32,
        )
        dq = exchange_rows(*dq)
        outs = [(kv_heads, jnp.bfloat16)] * peers
        dkv = exchange(add_parts(outs, own, total.reshape(own.shape)))
        dkv = [[piece] for piece in dkv]
    return unpack(me_ref, dq, dkv)


def solution(mesh):
    rows = P(("seq", "head"), None)
    in_specs = (rows, rows, rows, rows, rows, P("seq", "head"), P(None, "head", None))
    return jax.shard_map(
        body, mesh=mesh, in_specs=in_specs, out_specs=(rows, rows, rows), check_vma=False
    )
```

```python
import functools

import jax
import jax.numpy as jnp
from jax import lax
from jax.experimental import pallas as pl
from jax.experimental.pallas import tpu as pltpu
from jax.sharding import PartitionSpec as P

HD = 128
QB = 128
KB = 64
NSEL = 4
GROUP = 4
SCALE = HD ** (-0.5)
STAT = 16

VMEM = pl.BlockSpec(memory_space=pltpu.VMEM)
ANY = pl.BlockSpec(memory_space=pl.ANY)
HBM = pl.BlockSpec(memory_space=pltpu.HBM)
SMEM = pl.BlockSpec(memory_space=pltpu.SMEM)
NT = (((1,), (1,)), ((), ()))
TN = (((0,), (0,)), ((), ()))
PACK_PARAMS = pltpu.CompilerParams(vmem_limit_bytes=60 * 1024 * 1024)
PARAMS = pltpu.CompilerParams(vmem_limit_bytes=24 * 1024 * 1024)


def dot(a, b, dims=(((1,), (0,)), ((), ()))):
    return lax.dot_general(a, b, dims, preferred_element_type=jnp.float32)


def lanes(index, width):
    return pl.ds(pl.multiple_of(index * width, width), width)


def run_copies(pairs, sems):
    copies = [
        pltpu.make_async_copy(source, target, sems.at[i])
        for i, (source, target) in enumerate(pairs)
    ]
    for copy in copies:
        copy.start()
    return copies


def pack_kv_kernel(peers, me_ref, k_ref, v_ref, *refs):
    out_refs, sems = refs[:peers], refs[peers]
    kv_heads = out_refs[0].shape[0]
    pairs = []
    for c, out_ref in reversed(list(enumerate(out_refs))):
        for g in range(kv_heads):
            cols = lanes((me_ref[0] ^ c) * kv_heads + g, HD)
            pairs.append((k_ref.at[:, cols], out_ref.at[g, :, pl.ds(0, HD)]))
            pairs.append((v_ref.at[:, cols], out_ref.at[g, :, pl.ds(HD, HD)]))
    for copy in run_copies(pairs, sems):
        copy.wait()


def pack_kv(me, keys, values, peers):
    tokens, width = keys.shape
    kv_heads = width // HD // peers
    piece = jax.ShapeDtypeStruct((kv_heads, tokens, 2 * HD), jnp.bfloat16)
    return pl.pallas_call(
        functools.partial(pack_kv_kernel, peers),
        out_shape=(piece,) * peers,
        in_specs=[SMEM, HBM, HBM],
        out_specs=(VMEM,) * peers,
        scratch_shapes=[pltpu.SemaphoreType.DMA((2 * peers * kv_heads,))],
        compiler_params=PACK_PARAMS,
    )(me, keys, values)


def three_pieces(x):
    hi = x.astype(jnp.bfloat16)
    rest = x - hi.astype(jnp.float32)
    mid = rest.astype(jnp.bfloat16)
    low = (rest - mid.astype(jnp.float32)).astype(jnp.bfloat16)
    return hi, mid, low


def pack_q_kernel(peers, me_ref, q_any, do_any, o_any, *refs):
    half = peers // 2
    rows = refs[0].shape[0]
    out_refs = refs[:half] + tuple(refs[half].at[i * rows : (i + 1) * rows] for i in range(half))
    q_ref, do_ref, o_ref, sems = refs[half + 1 :]
    for copy in run_copies([(q_any, q_ref), (do_any, do_ref), (o_any, o_ref)], sems):
        copy.wait()
    heads = (out_refs[0].shape[0] - STAT) // KB
    lane = lax.broadcasted_iota(jnp.int32, (KB, HD), 1)
    delta = jnp.zeros((KB, HD), jnp.float32)
    for c, out_ref in enumerate(out_refs):
        for h in range(heads):
            cols = lanes((me_ref[0] ^ c) * heads + h, HD)
            do = do_ref[:, cols]
            out_ref[h * KB : (h + 1) * KB, :HD] = q_ref[:, cols]
            out_ref[h * KB : (h + 1) * KB, HD:] = do
            products = do.astype(jnp.float32) * o_ref[:, cols].astype(jnp.float32)
            total = jnp.sum(products, axis=-1, keepdims=True)
            delta = jnp.where(lane == c * heads + h, total, delta)
    by_head = delta.T
    for c, out_ref in enumerate(out_refs):
        hi, mid, low = three_pieces(by_head[c * heads : (c + 1) * heads])
        base = heads * KB
        zero = jnp.zeros((heads, HD - KB), jnp.bfloat16)
        first = jnp.concatenate([hi, zero, mid, zero], axis=1)
        second = jnp.concatenate([low, zero, zero, jnp.zeros_like(low)], axis=1)
        out_ref[base : base + STAT, :] = jnp.concatenate([first, second], axis=0)


def pack_q(me, queries, grad_out, outputs_saved, peers):
    tokens, width = queries.shape
    heads = width // HD // peers
    half = peers // 2
    rows = heads * tokens + STAT
    piece = jax.ShapeDtypeStruct((rows, 2 * HD), jnp.bfloat16)
    far = jax.ShapeDtypeStruct((half * rows, 2 * HD), jnp.bfloat16)
    return pl.pallas_call(
        functools.partial(pack_q_kernel, peers),
        out_shape=(piece,) * half + (far,),
        in_specs=[SMEM] + [HBM] * 3,
        out_specs=(VMEM,) * (half + 1),
        scratch_shapes=[pltpu.VMEM(queries.shape, jnp.bfloat16)] * 3
        + [pltpu.SemaphoreType.DMA((3,))],
        compiler_params=PACK_PARAMS,
    )(me, queries, grad_out, outputs_saved)


def query_rows(qdo, c, h):
    rows = slice(h * KB, (h + 1) * KB)
    pair = (qdo[c], qdo[c ^ 1])
    q = jnp.concatenate([ref[rows, :HD] for ref in pair], axis=0)
    do = jnp.concatenate([ref[rows, HD:] for ref in pair], axis=0)
    return q, do


def own_kernel(peers, me_ref, own_kv_ref, stats_ref, *refs):
    qdo = refs[:peers]
    listed_refs = refs[peers : 2 * peers]
    half = peers // 2
    *dq_refs, far_ref, own_ref = refs[2 * peers :]
    dq_refs += [far_ref.at[i * KB : (i + 1) * KB] for i in range(half)]
    heads = (qdo[0].shape[0] - STAT) // KB
    kv_heads = heads // GROUP
    key_row = lax.broadcasted_iota(jnp.int32, (QB, QB), 0)
    query_row = lax.broadcasted_iota(jnp.int32, (QB, QB), 1)
    swapped = jnp.where((me_ref[0] & 1) == 1, KB, 0)
    causal = (key_row ^ swapped) <= (query_row ^ swapped)
    for c in range(0, peers, 2):
        for g in range(kv_heads):
            own = [(c + i) * kv_heads + g for i in range(2)]
            kv = jnp.concatenate([own_kv_ref[u] for u in own], axis=0)
            k = kv[:, :HD]
            v = kv[:, HD:]
            dk = jnp.zeros((QB, HD), jnp.float32)
            dv = jnp.zeros((QB, HD), jnp.float32)
            for h in range(g * GROUP, (g + 1) * GROUP):
                q, do = query_rows(qdo, c, h)
                lse_row = stats_ref[0, h : h + 1, c * KB : c * KB + QB]
                delta_row = stats_ref[1, h : h + 1, c * KB : c * KB + QB]
                prob = jnp.where(causal, jnp.exp(dot(k, q, NT) * SCALE - lse_row), 0.0)
                score = (prob * (dot(v, do, NT) - delta_row)).astype(jnp.bfloat16)
                dq = dot(score, k, TN) * SCALE
                cols = slice(h * HD, (h + 1) * HD)
                for i in range(2):
                    part = listed_refs[c + i][:, cols] + dq[i * KB : (i + 1) * KB]
                    dq_refs[c + i][:, cols] = part.astype(jnp.bfloat16)
                dk += dot(score, q)
                dv += dot(prob.astype(jnp.bfloat16), do)
            for i in range(2):
                own_ref[own[i], :, :HD] = dk[i * KB : (i + 1) * KB] * SCALE
                own_ref[own[i], :, HD:] = dv[i * KB : (i + 1) * KB]


def own_terms(me, own_kv, stats, qdo, listed):
    peers = len(qdo)
    half = peers // 2
    rows, width = listed[0].shape
    piece = jax.ShapeDtypeStruct((rows, width), jnp.bfloat16)
    far = jax.ShapeDtypeStruct((half * rows, width), jnp.bfloat16)
    outs = pl.pallas_call(
        functools.partial(own_kernel, peers),
        out_shape=(piece,) * half + (far, jax.ShapeDtypeStruct(own_kv.shape, jnp.float32)),
        in_specs=[SMEM] + [VMEM] * (2 + 2 * peers),
        out_specs=(VMEM,) * (half + 2),
        compiler_params=PARAMS,
        cost_estimate=pl.CostEstimate(
            flops=335_000_000, bytes_accessed=4_000_000, transcendentals=260_000
        ),
    )(me, own_kv, stats, *qdo, *listed)
    return list(outs[:-1]), outs[-1]


def row_stats(me, qdo, lse_ref, stats_ref):
    peers = len(qdo)
    heads = (qdo[0].shape[0] - STAT) // KB
    base = heads * KB
    lse_blocks = [lse_ref[:, c * KB : (c + 1) * KB] for c in range(peers)]
    for c in range(peers):
        first = qdo[c][base : base + heads, :].astype(jnp.float32)
        second = qdo[c][base + heads : base + 2 * heads, :].astype(jnp.float32)
        delta = first[:, :KB] + first[:, HD : HD + KB] + second[:, :KB]
        lse_here = lse_blocks[0]
        for t in range(1, peers):
            lse_here = jnp.where((me ^ c) == t, lse_blocks[t], lse_here)
        stats_ref[0, :, c * KB : (c + 1) * KB] = lse_here
        stats_ref[1, :, c * KB : (c + 1) * KB] = delta


def listed_kernel(peers, me_ref, slot_ref, lse_ref, kv, *refs):
    qdo, outs, sums = refs[:peers], refs[peers:-1], refs[-1]
    stats_ref, dq_refs, part_refs = outs[0], outs[1 : peers + 1], outs[peers + 1 :]
    row_stats(me_ref[0], qdo, lse_ref, stats_ref)
    heads = (qdo[0].shape[0] - STAT) // KB
    sums[...] = jnp.zeros_like(sums)

    def scores(c, h):
        q, do = query_rows(qdo, c, h)
        slots = [slot_ref[(c // 2 * heads + h) * NSEL + n] for n in range(NSEL)]
        rows_kv = jnp.concatenate([kv[s] for s in slots], axis=0)
        k = rows_kv[:, :HD]
        v = rows_kv[:, HD:]
        lse_row = stats_ref[0, h : h + 1, c * KB : c * KB + QB]
        delta_row = stats_ref[1, h : h + 1, c * KB : c * KB + QB]
        prob = jnp.exp(dot(k, q, NT) * SCALE - lse_row)
        score = (prob * (dot(v, do, NT) - delta_row)).astype(jnp.bfloat16)
        return c, h, slots, q, do, k, prob.astype(jnp.bfloat16), score

    def gradients(c, h, slots, q, do, k, prob, score):
        dq = dot(score, k, TN) * SCALE
        cols = slice(h * HD, (h + 1) * HD)
        for i in range(2):
            dq_refs[c + i][:, cols] = dq[i * KB : (i + 1) * KB]
        dk = dot(score, q) * SCALE
        dv = dot(prob, do)
        for n in range(NSEL):
            part = slice(n * KB, (n + 1) * KB)
            sums[slots[n], :, :HD] += dk[part]
            sums[slots[n], :, HD:] += dv[part]

    waiting = []
    for c in range(0, peers, 2):
        for h in range(heads):
            waiting.append(scores(c, h))
            if len(waiting) > 2:
                gradients(*waiting.pop(0))
    for state in waiting:
        gradients(*state)
    first = 0
    for part_ref in part_refs:
        part_ref[...] = sums[first : first + part_ref.shape[0]].astype(part_ref.dtype)
        first += part_ref.shape[0]


def listed_terms(me, slots, lse, kv, qdo, parts):
    peers = len(qdo)
    heads, tokens = lse.shape
    outs = pl.pallas_call(
        functools.partial(listed_kernel, peers),
        out_shape=(
            jax.ShapeDtypeStruct((2, heads, tokens), jnp.float32),
            *[jax.ShapeDtypeStruct((KB, heads * HD), jnp.float32)] * peers,
            *[jax.ShapeDtypeStruct((units,) + kv.shape[1:], kind) for units, kind in parts],
        ),
        in_specs=[SMEM, SMEM] + [VMEM] * (2 + peers),
        out_specs=(VMEM,) * (1 + peers + len(parts)),
        scratch_shapes=[pltpu.VMEM(kv.shape, jnp.float32)],
        compiler_params=PARAMS,
        cost_estimate=pl.CostEstimate(
            flops=671_000_000, bytes_accessed=8_000_000, transcendentals=530_000
        ),
    )(me, slots, lse, kv, *qdo)
    return outs[0], outs[1 : peers + 1], outs[peers + 1 :]


def add_kernel(firsts, *refs):
    terms, out_refs = refs[: len(firsts)], refs[len(firsts) :]
    done = 0
    for out_ref in out_refs:
        size = out_ref.shape[0]
        total = None
        for ref, first in zip(terms, firsts):
            part = ref[first + done : first + done + size].astype(jnp.float32)
            total = part if total is None else total + part
        out_ref[...] = total.astype(out_ref.dtype)
        done += size


def add_parts(outs, *terms, bytes_moved=2_000_000):
    terms = [term if isinstance(term, tuple) else (term, 0) for term in terms]
    arrays = [array for array, _ in terms]
    tail = arrays[0].shape[1:]
    return pl.pallas_call(
        functools.partial(add_kernel, [first for _, first in terms]),
        out_shape=[jax.ShapeDtypeStruct((size,) + tail, kind) for size, kind in outs],
        in_specs=[VMEM] * len(arrays),
        out_specs=[VMEM] * len(outs),
        compiler_params=PARAMS,
        cost_estimate=pl.CostEstimate(
            flops=2_000_000, bytes_accessed=bytes_moved, transcendentals=0
        ),
    )(*arrays)


def add_rounded(units, *terms):
    return add_parts([(units, jnp.bfloat16)], *terms)[0]


def unpack_q_kernel(peers, me_ref, *refs):
    gq_ref = refs[peers]
    width = refs[0].shape[1]
    for c in range(peers):
        gq_ref[:, lanes(me_ref[0] ^ c, width)] = refs[c][...]


def unpack_kv_kernel(counts, me_ref, *refs):
    *term_refs, gk_ref, gv_ref = refs
    kv_heads = refs[0].shape[0]
    at = 0
    for c, count in enumerate(counts):
        terms = term_refs[at : at + count]
        at += count
        for g in range(kv_heads):
            cols = lanes((me_ref[0] ^ c) * kv_heads + g, HD)
            total = terms[0][g]
            if count > 1:
                total = sum(term[g].astype(jnp.float32) for term in terms).astype(jnp.bfloat16)
            gk_ref[:, cols] = total[:, :HD]
            gv_ref[:, cols] = total[:, HD:]


def unpack(me, dq, dkv):
    peers = len(dq)
    tokens, width = dq[0].shape
    kv_width = dkv[0][0].shape[0] * peers * HD
    grad_q = pl.pallas_call(
        functools.partial(unpack_q_kernel, peers),
        out_shape=jax.ShapeDtypeStruct((tokens, peers * width), jnp.bfloat16),
        in_specs=[SMEM] + [VMEM] * peers,
        out_specs=VMEM,
        compiler_params=PARAMS,
    )(me, *dq)
    flat = [term for terms in dkv for term in terms]
    grad_q, flat[0] = lax.optimization_barrier((grad_q, flat[0]))
    grad_k, grad_v = pl.pallas_call(
        functools.partial(unpack_kv_kernel, [len(terms) for terms in dkv]),
        out_shape=(jax.ShapeDtypeStruct((tokens, kv_width), jnp.bfloat16),) * 2,
        in_specs=[SMEM] + [VMEM] * len(flat),
        out_specs=(VMEM, VMEM),
        compiler_params=PARAMS,
    )(me, *flat)
    return grad_q, grad_k, grad_v


def exchange(pieces):
    peers = len(pieces)
    moved = [
        lax.ppermute(pieces[c], "head", [(h, h ^ c) for h in range(peers)])
        for c in range(1, peers)
    ]
    return [pieces[0]] + moved


def exchange_cores(here, near, far):
    rows = here.shape[0]
    flip = [(h, h ^ 1) for h in range(4)]
    near = lax.ppermute(near, "head", flip)
    return [here, near, far[:rows], lax.ppermute(far[rows:], "head", flip)]


def exchange_rows(here, near, far):
    across = [(h, h ^ 2) for h in range(4)]
    return exchange_cores(here, near, lax.ppermute(far, "head", across))


def send_back(piece, c, shards, peers):
    pairs = [
        (s * peers + h, (s - 2) % shards * peers + (h ^ c))
        for s in range(shards)
        for h in range(peers)
    ]
    return lax.ppermute(piece, ("seq", "head"), pairs)


def body(queries, keys, values, outputs_saved, grad_out, lse, block_lists):
    peers = lax.axis_size("head")
    shards = lax.axis_size("seq")
    me = lax.axis_index("seq")
    head_me = lax.axis_index("head")
    me_ref = head_me.astype(jnp.int32).reshape(1)
    heads = lse.shape[1]
    kv_heads = heads // GROUP
    key_count = peers
    units = key_count * kv_heads

    kv_pack = pack_kv(me_ref, keys, values, peers)
    own_kv = jnp.concatenate(exchange(kv_pack), axis=0)

    per_peer = block_lists.reshape(shards, -1)
    requests = per_peer.shape[1]
    order = jnp.arange(requests, dtype=jnp.int32)
    group_of = order % (heads * NSEL) // (NSEL * GROUP)
    block_turn = jnp.where(head_me >= peers // 2, requests // 2, 0)
    capacity = -(-requests // (shards - 1))
    dense = units <= capacity and shards == 8

    if dense:
        far = shards // 2
        swap = [(s, s ^ 1) for s in range(shards)]
        ahead = [(s, (s + 2) % shards) for s in range(shards)]
        back = [(s, (s - 2) % shards) for s in range(shards)]
        same1 = lax.ppermute(own_kv, "seq", ahead)
        cross0 = lax.ppermute(own_kv, "seq", swap)
        later_me, held = lax.optimization_barrier((me_ref, own_kv))
        q_pieces = pack_q(later_me, queries, grad_out, outputs_saved, peers)
        per_peer, q_pieces = lax.optimization_barrier((per_peer, q_pieces))
        qdo = exchange_rows(*q_pieces)
        mine = lax.dynamic_index_in_dim(per_peer, me, 0, keepdims=False)
        owner = mine // key_count
        apart = (me // 2 - owner // 2) % far
        crossed = (me ^ owner) & 1
        piece = jnp.where(crossed == 1, far - 1 + (apart + 1) % far, apart - 1)
        slots = piece * units + (mine % key_count ^ head_me) * kv_heads + group_of
        slots = jnp.roll(slots, block_turn)
        held, slots = lax.optimization_barrier((held, slots))
        same3 = lax.ppermute(held, "seq", back)
        same2 = lax.ppermute(same1, "seq", ahead)
        cross1 = lax.ppermute(same1, "seq", swap)
        cross3 = lax.ppermute(same3, "seq", swap)
        held, cross1 = lax.optimization_barrier((same2, cross1))
        cross2 = lax.ppermute(held, "seq", swap)
        kv_all = jnp.zeros((7 * units,) + own_kv.shape[1:], jnp.bfloat16)
        arriving = [(same1, 0), (cross0, 4), (cross1, 5), (same2, 1), (same3, 2)]
        for array, at in arriving + [(cross2, 6), (cross3, 3)]:
            kv_all = lax.dynamic_update_slice_in_dim(kv_all, array, at * units, 0)
        wide, low = jnp.float32, jnp.bfloat16
        part_types = [(1, wide), (1, wide), (2, low), (1, wide), (1, low), (1, low)]
        part_types = [(count * units, kind) for count, kind in part_types]
    else:
        owner = per_peer // key_count
        earlier = (owner[:, :, None] == owner[:, None, :]) & (order[None, :] < order[:, None])
        position = jnp.sum(earlier.astype(jnp.int32), axis=2)
        slots = lax.dynamic_index_in_dim(owner * capacity + position, me, 0, keepdims=False)
        hits = (owner == me)[:, :, None] & (position[:, :, None] == jnp.arange(capacity))
        hits = hits.astype(jnp.int32)
        used = jnp.sum(hits, axis=1).reshape(-1)
        wanted = (per_peer % key_count ^ head_me) * kv_heads + group_of[None, :]
        wanted = jnp.sum(hits * wanted[:, :, None], axis=1).reshape(-1)
        kv_all = lax.all_to_all(own_kv[wanted], "seq", 0, 0, tiled=True)
        part_types = [(kv_all.shape[0], jnp.bfloat16)]
        slots = jnp.roll(slots, block_turn)
        qdo = exchange_rows(*pack_q(me_ref, queries, grad_out, outputs_saved, peers))

    stats, listed, parts = listed_terms(me_ref, slots, lse.T, kv_all, qdo, part_types)
    dq, own = own_terms(me_ref, own_kv, stats, qdo, listed)

    if dense:
        stay1, stay2, away3, leave0, leave1, leave2 = parts
        came2 = lax.ppermute(leave2, "seq", swap)
        came3 = lax.ppermute(away3, "seq", ahead)
        came1 = lax.ppermute(leave1, "seq", swap)
        hop = lax.ppermute(add_rounded(units, stay2, came2), "seq", back)
        across = [(h, h ^ 2) for h in range(peers)]
        dq[2] = lax.ppermute(dq[2], "head", across)
        came3, dq[2] = lax.optimization_barrier((came3, dq[2]))
        near = add_rounded(units, leave0, (came3, units))
        came0 = lax.ppermute(near, "seq", swap)
        half, pair = units // 2, units // peers
        outs = [(half, wide), (pair, low), (pair, low)]
        base, *base_far = add_parts(outs, own, came3, came0, bytes_moved=16_000_000)
        base, dq = lax.optimization_barrier((base, dq))
        outs = [(half, low), (pair, low), (pair, low)]
        side, *side_far = add_parts(outs, stay1, came1, hop)
        side_far = [send_back(piece, c, shards, peers) for c, piece in zip((2, 3), side_far)]
        side = lax.ppermute(side, "seq", back)
        dq = exchange_cores(*dq)
        base_far = [
            lax.ppermute(piece, "head", [(h, h ^ c) for h in range(peers)])
            for c, piece in zip((2, 3), base_far)
        ]
        side, base_far, side_far = lax.optimization_barrier((side, base_far, side_far))
        here, near = add_parts([(pair, low)] * 2, base, side)
        near = lax.ppermute(near, "head", [(h, h ^ 1) for h in range(peers)])
        dkv = [[here], [near]] + [list(terms) for terms in zip(base_far, side_far)]
    else:
        parts = lax.all_to_all(parts[0], "seq", 0, 0, tiled=True)
        chosen = (jnp.arange(units)[:, None] == wanted[None, :]) & (used[None, :] > 0)
        total = jnp.dot(
            chosen.astype(jnp.bfloat16),
            parts.reshape(parts.shape[0], -1),
            preferred_element_type=jnp.float32,
        )
        dq = exchange_rows(*dq)
        outs = [(kv_heads, jnp.bfloat16)] * peers
        dkv = exchange(add_parts(outs, own, total.reshape(own.shape)))
        dkv = [[piece] for piece in dkv]
    return unpack(me_ref, dq, dkv)


def solution(mesh):
    rows = P(("seq", "head"), None)
    in_specs = (rows, rows, rows, rows, rows, P("seq", "head"), P(None, "head", None))
    return jax.shard_map(
        body, mesh=mesh, in_specs=in_specs, out_specs=(rows, rows, rows), check_vma=False
    )
```

```python
import functools

import jax
import jax.numpy as jnp
from jax import lax
from jax.experimental import pallas as pl
from jax.experimental.pallas import tpu as pltpu
from jax.sharding import PartitionSpec as P

HD = 128
QB = 128
KB = 64
NSEL = 4
GROUP = 4
SCALE = HD ** (-0.5)
STAT = 16

VMEM = pl.BlockSpec(memory_space=pltpu.VMEM)
ANY = pl.BlockSpec(memory_space=pl.ANY)
HBM = pl.BlockSpec(memory_space=pltpu.HBM)
SMEM = pl.BlockSpec(memory_space=pltpu.SMEM)
NT = (((1,), (1,)), ((), ()))
TN = (((0,), (0,)), ((), ()))
PACK_PARAMS = pltpu.CompilerParams(vmem_limit_bytes=60 * 1024 * 1024)
PARAMS = pltpu.CompilerParams(vmem_limit_bytes=24 * 1024 * 1024)


def dot(a, b, dims=(((1,), (0,)), ((), ()))):
    return lax.dot_general(a, b, dims, preferred_element_type=jnp.float32)


def lanes(index, width):
    return pl.ds(pl.multiple_of(index * width, width), width)


def run_copies(pairs, sems):
    copies = [
        pltpu.make_async_copy(source, target, sems.at[i])
        for i, (source, target) in enumerate(pairs)
    ]
    for copy in copies:
        copy.start()
    return copies


def pack_kv_kernel(peers, me_ref, k_ref, v_ref, *refs):
    out_refs, sems = refs[:peers], refs[peers]
    kv_heads = out_refs[0].shape[0]
    pairs = []
    for c, out_ref in reversed(list(enumerate(out_refs))):
        for g in range(kv_heads):
            cols = lanes((me_ref[0] ^ c) * kv_heads + g, HD)
            pairs.append((k_ref.at[:, cols], out_ref.at[g, :, pl.ds(0, HD)]))
            pairs.append((v_ref.at[:, cols], out_ref.at[g, :, pl.ds(HD, HD)]))
    for copy in run_copies(pairs, sems):
        copy.wait()


def pack_kv(me, keys, values, peers):
    tokens, width = keys.shape
    kv_heads = width // HD // peers
    piece = jax.ShapeDtypeStruct((kv_heads, tokens, 2 * HD), jnp.bfloat16)
    return pl.pallas_call(
        functools.partial(pack_kv_kernel, peers),
        out_shape=(piece,) * peers,
        in_specs=[SMEM, HBM, HBM],
        out_specs=(VMEM,) * peers,
        scratch_shapes=[pltpu.SemaphoreType.DMA((2 * peers * kv_heads,))],
        compiler_params=PACK_PARAMS,
    )(me, keys, values)


def three_pieces(x):
    hi = x.astype(jnp.bfloat16)
    rest = x - hi.astype(jnp.float32)
    mid = rest.astype(jnp.bfloat16)
    low = (rest - mid.astype(jnp.float32)).astype(jnp.bfloat16)
    return hi, mid, low


def pack_q_kernel(peers, me_ref, q_any, do_any, o_any, *refs):
    half = peers // 2
    rows = refs[0].shape[0]
    out_refs = refs[:half] + tuple(refs[half].at[i * rows : (i + 1) * rows] for i in range(half))
    q_ref, do_ref, o_ref, sems = refs[half + 1 :]
    for copy in run_copies([(q_any, q_ref), (do_any, do_ref), (o_any, o_ref)], sems):
        copy.wait()
    heads = (out_refs[0].shape[0] - STAT) // KB
    lane = lax.broadcasted_iota(jnp.int32, (KB, HD), 1)
    delta = jnp.zeros((KB, HD), jnp.float32)
    for c, out_ref in enumerate(out_refs):
        for h in range(heads):
            cols = lanes((me_ref[0] ^ c) * heads + h, HD)
            do = do_ref[:, cols]
            out_ref[h * KB : (h + 1) * KB, :HD] = q_ref[:, cols]
            out_ref[h * KB : (h + 1) * KB, HD:] = do
            products = do.astype(jnp.float32) * o_ref[:, cols].astype(jnp.float32)
            total = jnp.sum(products, axis=-1, keepdims=True)
            delta = jnp.where(lane == c * heads + h, total, delta)
    by_head = delta.T
    for c, out_ref in enumerate(out_refs):
        hi, mid, low = three_pieces(by_head[c * heads : (c + 1) * heads])
        base = heads * KB
        zero = jnp.zeros((heads, HD - KB), jnp.bfloat16)
        first = jnp.concatenate([hi, zero, mid, zero], axis=1)
        second = jnp.concatenate([low, zero, zero, jnp.zeros_like(low)], axis=1)
        out_ref[base : base + STAT, :] = jnp.concatenate([first, second], axis=0)


def pack_q(me, queries, grad_out, outputs_saved, peers):
    tokens, width = queries.shape
    heads = width // HD // peers
    half = peers // 2
    rows = heads * tokens + STAT
    piece = jax.ShapeDtypeStruct((rows, 2 * HD), jnp.bfloat16)
    far = jax.ShapeDtypeStruct((half * rows, 2 * HD), jnp.bfloat16)
    return pl.pallas_call(
        functools.partial(pack_q_kernel, peers),
        out_shape=(piece,) * half + (far,),
        in_specs=[SMEM] + [HBM] * 3,
        out_specs=(VMEM,) * (half + 1),
        scratch_shapes=[pltpu.VMEM(queries.shape, jnp.bfloat16)] * 3
        + [pltpu.SemaphoreType.DMA((3,))],
        compiler_params=PACK_PARAMS,
    )(me, queries, grad_out, outputs_saved)


def query_rows(qdo, c, h):
    rows = slice(h * KB, (h + 1) * KB)
    pair = (qdo[c], qdo[c ^ 1])
    q = jnp.concatenate([ref[rows, :HD] for ref in pair], axis=0)
    do = jnp.concatenate([ref[rows, HD:] for ref in pair], axis=0)
    return q, do


def own_kernel(peers, me_ref, own_kv_ref, stats_ref, *refs):
    qdo = refs[:peers]
    listed_refs = refs[peers : 2 * peers]
    half = peers // 2
    *dq_refs, far_ref, own_ref = refs[2 * peers :]
    dq_refs += [far_ref.at[i * KB : (i + 1) * KB] for i in range(half)]
    heads = (qdo[0].shape[0] - STAT) // KB
    kv_heads = heads // GROUP
    key_row = lax.broadcasted_iota(jnp.int32, (QB, QB), 0)
    query_row = lax.broadcasted_iota(jnp.int32, (QB, QB), 1)
    swapped = jnp.where((me_ref[0] & 1) == 1, KB, 0)
    causal = (key_row ^ swapped) <= (query_row ^ swapped)
    for c in range(0, peers, 2):
        for g in range(kv_heads):
            own = [(c + i) * kv_heads + g for i in range(2)]
            kv = jnp.concatenate([own_kv_ref[u] for u in own], axis=0)
            k = kv[:, :HD]
            v = kv[:, HD:]
            dk = jnp.zeros((QB, HD), jnp.float32)
            dv = jnp.zeros((QB, HD), jnp.float32)
            for h in range(g * GROUP, (g + 1) * GROUP):
                q, do = query_rows(qdo, c, h)
                lse_row = stats_ref[0, h : h + 1, c * KB : c * KB + QB]
                delta_row = stats_ref[1, h : h + 1, c * KB : c * KB + QB]
                prob = jnp.where(causal, jnp.exp(dot(k, q, NT) * SCALE - lse_row), 0.0)
                score = (prob * (dot(v, do, NT) - delta_row)).astype(jnp.bfloat16)
                dq = dot(score, k, TN) * SCALE
                cols = slice(h * HD, (h + 1) * HD)
                for i in range(2):
                    part = listed_refs[c + i][:, cols] + dq[i * KB : (i + 1) * KB]
                    dq_refs[c + i][:, cols] = part.astype(jnp.bfloat16)
                dk += dot(score, q)
                dv += dot(prob.astype(jnp.bfloat16), do)
            for i in range(2):
                own_ref[own[i], :, :HD] = dk[i * KB : (i + 1) * KB] * SCALE
                own_ref[own[i], :, HD:] = dv[i * KB : (i + 1) * KB]


def own_terms(me, own_kv, stats, qdo, listed):
    peers = len(qdo)
    half = peers // 2
    rows, width = listed[0].shape
    piece = jax.ShapeDtypeStruct((rows, width), jnp.bfloat16)
    far = jax.ShapeDtypeStruct((half * rows, width), jnp.bfloat16)
    outs = pl.pallas_call(
        functools.partial(own_kernel, peers),
        out_shape=(piece,) * half + (far, jax.ShapeDtypeStruct(own_kv.shape, jnp.float32)),
        in_specs=[SMEM] + [VMEM] * (2 + 2 * peers),
        out_specs=(VMEM,) * (half + 2),
        compiler_params=PARAMS,
        cost_estimate=pl.CostEstimate(
            flops=335_000_000, bytes_accessed=4_000_000, transcendentals=260_000
        ),
    )(me, own_kv, stats, *qdo, *listed)
    return list(outs[:-1]), outs[-1]


def row_stats(me, qdo, lse_ref, stats_ref):
    peers = len(qdo)
    heads = (qdo[0].shape[0] - STAT) // KB
    base = heads * KB
    lse_blocks = [lse_ref[:, c * KB : (c + 1) * KB] for c in range(peers)]
    for c in range(peers):
        first = qdo[c][base : base + heads, :].astype(jnp.float32)
        second = qdo[c][base + heads : base + 2 * heads, :].astype(jnp.float32)
        delta = first[:, :KB] + first[:, HD : HD + KB] + second[:, :KB]
        lse_here = lse_blocks[0]
        for t in range(1, peers):
            lse_here = jnp.where((me ^ c) == t, lse_blocks[t], lse_here)
        stats_ref[0, :, c * KB : (c + 1) * KB] = lse_here
        stats_ref[1, :, c * KB : (c + 1) * KB] = delta


def listed_kernel(peers, me_ref, slot_ref, lse_ref, kv, *refs):
    qdo, outs, sums = refs[:peers], refs[peers:-1], refs[-1]
    stats_ref, dq_refs, part_refs = outs[0], outs[1 : peers + 1], outs[peers + 1 :]
    row_stats(me_ref[0], qdo, lse_ref, stats_ref)
    heads = (qdo[0].shape[0] - STAT) // KB
    sums[...] = jnp.zeros_like(sums)

    def scores(c, h):
        q, do = query_rows(qdo, c, h)
        slots = [slot_ref[(c // 2 * heads + h) * NSEL + n] for n in range(NSEL)]
        rows_kv = jnp.concatenate([kv[s] for s in slots], axis=0)
        k = rows_kv[:, :HD]
        v = rows_kv[:, HD:]
        lse_row = stats_ref[0, h : h + 1, c * KB : c * KB + QB]
        delta_row = stats_ref[1, h : h + 1, c * KB : c * KB + QB]
        prob = jnp.exp(dot(k, q, NT) * SCALE - lse_row)
        score = (prob * (dot(v, do, NT) - delta_row)).astype(jnp.bfloat16)
        return c, h, slots, q, do, k, prob.astype(jnp.bfloat16), score

    def gradients(c, h, slots, q, do, k, prob, score):
        dq = dot(score, k, TN) * SCALE
        cols = slice(h * HD, (h + 1) * HD)
        for i in range(2):
            dq_refs[c + i][:, cols] = dq[i * KB : (i + 1) * KB]
        dk = dot(score, q) * SCALE
        dv = dot(prob, do)
        for n in range(NSEL):
            part = slice(n * KB, (n + 1) * KB)
            sums[slots[n], :, :HD] += dk[part]
            sums[slots[n], :, HD:] += dv[part]

    waiting = []
    for c in range(0, peers, 2):
        for h in range(heads):
            waiting.append(scores(c, h))
            if len(waiting) > 2:
                gradients(*waiting.pop(0))
    for state in waiting:
        gradients(*state)
    first = 0
    for part_ref in part_refs:
        part_ref[...] = sums[first : first + part_ref.shape[0]].astype(part_ref.dtype)
        first += part_ref.shape[0]


def listed_terms(me, slots, lse, kv, qdo, parts):
    peers = len(qdo)
    heads, tokens = lse.shape
    outs = pl.pallas_call(
        functools.partial(listed_kernel, peers),
        out_shape=(
            jax.ShapeDtypeStruct((2, heads, tokens), jnp.float32),
            *[jax.ShapeDtypeStruct((KB, heads * HD), jnp.float32)] * peers,
            *[jax.ShapeDtypeStruct((units,) + kv.shape[1:], kind) for units, kind in parts],
        ),
        in_specs=[SMEM, SMEM] + [VMEM] * (2 + peers),
        out_specs=(VMEM,) * (1 + peers + len(parts)),
        scratch_shapes=[pltpu.VMEM(kv.shape, jnp.float32)],
        compiler_params=PARAMS,
        cost_estimate=pl.CostEstimate(
            flops=671_000_000, bytes_accessed=8_000_000, transcendentals=530_000
        ),
    )(me, slots, lse, kv, *qdo)
    return outs[0], outs[1 : peers + 1], outs[peers + 1 :]


def add_kernel(firsts, *refs):
    terms, out_refs = refs[: len(firsts)], refs[len(firsts) :]
    done = 0
    for out_ref in out_refs:
        size = out_ref.shape[0]
        total = None
        for ref, first in zip(terms, firsts):
            part = ref[first + done : first + done + size].astype(jnp.float32)
            total = part if total is None else total + part
        out_ref[...] = total.astype(out_ref.dtype)
        done += size


def add_parts(outs, *terms, bytes_moved=2_000_000):
    terms = [term if isinstance(term, tuple) else (term, 0) for term in terms]
    arrays = [array for array, _ in terms]
    tail = arrays[0].shape[1:]
    return pl.pallas_call(
        functools.partial(add_kernel, [first for _, first in terms]),
        out_shape=[jax.ShapeDtypeStruct((size,) + tail, kind) for size, kind in outs],
        in_specs=[VMEM] * len(arrays),
        out_specs=[VMEM] * len(outs),
        compiler_params=PARAMS,
        cost_estimate=pl.CostEstimate(
            flops=2_000_000, bytes_accessed=bytes_moved, transcendentals=0
        ),
    )(*arrays)


def add_rounded(units, *terms):
    return add_parts([(units, jnp.bfloat16)], *terms)[0]


def unpack_q_kernel(peers, me_ref, *refs):
    gq_ref = refs[peers]
    width = refs[0].shape[1]
    for c in range(peers):
        gq_ref[:, lanes(me_ref[0] ^ c, width)] = refs[c][...]


def unpack_kv_kernel(counts, me_ref, *refs):
    *term_refs, gk_ref, gv_ref = refs
    kv_heads = refs[0].shape[0]
    at = 0
    for c, count in enumerate(counts):
        terms = term_refs[at : at + count]
        at += count
        for g in range(kv_heads):
            cols = lanes((me_ref[0] ^ c) * kv_heads + g, HD)
            total = terms[0][g]
            if count > 1:
                total = sum(term[g].astype(jnp.float32) for term in terms).astype(jnp.bfloat16)
            gk_ref[:, cols] = total[:, :HD]
            gv_ref[:, cols] = total[:, HD:]


def unpack(me, dq, dkv):
    peers = len(dq)
    tokens, width = dq[0].shape
    kv_width = dkv[0][0].shape[0] * peers * HD
    grad_q = pl.pallas_call(
        functools.partial(unpack_q_kernel, peers),
        out_shape=jax.ShapeDtypeStruct((tokens, peers * width), jnp.bfloat16),
        in_specs=[SMEM] + [VMEM] * peers,
        out_specs=VMEM,
        compiler_params=PARAMS,
    )(me, *dq)
    flat = [term for terms in dkv for term in terms]
    grad_q, flat[0] = lax.optimization_barrier((grad_q, flat[0]))
    grad_k, grad_v = pl.pallas_call(
        functools.partial(unpack_kv_kernel, [len(terms) for terms in dkv]),
        out_shape=(jax.ShapeDtypeStruct((tokens, kv_width), jnp.bfloat16),) * 2,
        in_specs=[SMEM] + [VMEM] * len(flat),
        out_specs=(VMEM, VMEM),
        compiler_params=PARAMS,
    )(me, *flat)
    return grad_q, grad_k, grad_v


def exchange(pieces):
    peers = len(pieces)
    moved = [
        lax.ppermute(pieces[c], "head", [(h, h ^ c) for h in range(peers)])
        for c in range(1, peers)
    ]
    return [pieces[0]] + moved


def exchange_cores(here, near, far):
    rows = here.shape[0]
    flip = [(h, h ^ 1) for h in range(4)]
    near = lax.ppermute(near, "head", flip)
    return [here, near, far[:rows], lax.ppermute(far[rows:], "head", flip)]


def exchange_rows(here, near, far):
    across = [(h, h ^ 2) for h in range(4)]
    return exchange_cores(here, near, lax.ppermute(far, "head", across))


def send_back(piece, c, shards, peers):
    pairs = [
        (s * peers + h, (s - 2) % shards * peers + (h ^ c))
        for s in range(shards)
        for h in range(peers)
    ]
    return lax.ppermute(piece, ("seq", "head"), pairs)


def body(queries, keys, values, outputs_saved, grad_out, lse, block_lists):
    peers = lax.axis_size("head")
    shards = lax.axis_size("seq")
    me = lax.axis_index("seq")
    head_me = lax.axis_index("head")
    me_ref = head_me.astype(jnp.int32).reshape(1)
    heads = lse.shape[1]
    kv_heads = heads // GROUP
    key_count = peers
    units = key_count * kv_heads

    kv_pack = pack_kv(me_ref, keys, values, peers)
    own_kv = jnp.concatenate(exchange(kv_pack), axis=0)

    per_peer = block_lists.reshape(shards, -1)
    requests = per_peer.shape[1]
    order = jnp.arange(requests, dtype=jnp.int32)
    group_of = order % (heads * NSEL) // (NSEL * GROUP)
    block_turn = jnp.where(head_me >= peers // 2, requests // 2, 0)
    capacity = -(-requests // (shards - 1))
    dense = units <= capacity and shards == 8

    if dense:
        far = shards // 2
        swap = [(s, s ^ 1) for s in range(shards)]
        ahead = [(s, (s + 2) % shards) for s in range(shards)]
        back = [(s, (s - 2) % shards) for s in range(shards)]
        same1 = lax.ppermute(own_kv, "seq", ahead)
        cross0 = lax.ppermute(own_kv, "seq", swap)
        later_me, held = lax.optimization_barrier((me_ref, own_kv))
        q_pieces = pack_q(later_me, queries, grad_out, outputs_saved, peers)
        held, q_pieces = lax.optimization_barrier((held, q_pieces))
        same3 = lax.ppermute(held, "seq", back)
        qdo = exchange_rows(*q_pieces)
        per_peer, same1 = lax.optimization_barrier((per_peer, same1))
        mine = lax.dynamic_index_in_dim(per_peer, me, 0, keepdims=False)
        owner = mine // key_count
        apart = (me // 2 - owner // 2) % far
        crossed = (me ^ owner) & 1
        piece = jnp.where(crossed == 1, far - 1 + (apart + 1) % far, apart - 1)
        slots = piece * units + (mine % key_count ^ head_me) * kv_heads + group_of
        slots = jnp.roll(slots, block_turn)
        same2 = lax.ppermute(same1, "seq", ahead)
        cross1 = lax.ppermute(same1, "seq", swap)
        cross3 = lax.ppermute(same3, "seq", swap)
        held, cross1 = lax.optimization_barrier((same2, cross1))
        cross2 = lax.ppermute(held, "seq", swap)
        kv_all = jnp.zeros((7 * units,) + own_kv.shape[1:], jnp.bfloat16)
        arriving = [(same1, 0), (cross0, 4), (cross1, 5), (same2, 1), (same3, 2)]
        for array, at in arriving + [(cross2, 6), (cross3, 3)]:
            kv_all = lax.dynamic_update_slice_in_dim(kv_all, array, at * units, 0)
        wide, low = jnp.float32, jnp.bfloat16
        part_types = [(1, wide), (1, wide), (2, low), (1, wide), (1, low), (1, low)]
        part_types = [(count * units, kind) for count, kind in part_types]
    else:
        owner = per_peer // key_count
        earlier = (owner[:, :, None] == owner[:, None, :]) & (order[None, :] < order[:, None])
        position = jnp.sum(earlier.astype(jnp.int32), axis=2)
        slots = lax.dynamic_index_in_dim(owner * capacity + position, me, 0, keepdims=False)
        hits = (owner == me)[:, :, None] & (position[:, :, None] == jnp.arange(capacity))
        hits = hits.astype(jnp.int32)
        used = jnp.sum(hits, axis=1).reshape(-1)
        wanted = (per_peer % key_count ^ head_me) * kv_heads + group_of[None, :]
        wanted = jnp.sum(hits * wanted[:, :, None], axis=1).reshape(-1)
        kv_all = lax.all_to_all(own_kv[wanted], "seq", 0, 0, tiled=True)
        part_types = [(kv_all.shape[0], jnp.bfloat16)]
        slots = jnp.roll(slots, block_turn)
        qdo = exchange_rows(*pack_q(me_ref, queries, grad_out, outputs_saved, peers))

    stats, listed, parts = listed_terms(me_ref, slots, lse.T, kv_all, qdo, part_types)
    dq, own = own_terms(me_ref, own_kv, stats, qdo, listed)

    if dense:
        stay1, stay2, away3, leave0, leave1, leave2 = parts
        came2 = lax.ppermute(leave2, "seq", swap)
        came3 = lax.ppermute(away3, "seq", ahead)
        came1 = lax.ppermute(leave1, "seq", swap)
        hop = lax.ppermute(add_rounded(units, stay2, came2), "seq", back)
        across = [(h, h ^ 2) for h in range(peers)]
        dq[2] = lax.ppermute(dq[2], "head", across)
        came3, dq[2] = lax.optimization_barrier((came3, dq[2]))
        near = add_rounded(units, leave0, (came3, units))
        came0 = lax.ppermute(near, "seq", swap)
        half, pair = units // 2, units // peers
        outs = [(half, wide), (pair, low), (pair, low)]
        base, *base_far = add_parts(outs, own, came3, came0, bytes_moved=16_000_000)
        base, dq = lax.optimization_barrier((base, dq))
        outs = [(half, low), (pair, low), (pair, low)]
        side, *side_far = add_parts(outs, stay1, came1, hop)
        side_far = [send_back(piece, c, shards, peers) for c, piece in zip((2, 3), side_far)]
        side = lax.ppermute(side, "seq", back)
        dq = exchange_cores(*dq)
        base_far = [
            lax.ppermute(piece, "head", [(h, h ^ c) for h in range(peers)])
            for c, piece in zip((2, 3), base_far)
        ]
        side, base_far, side_far = lax.optimization_barrier((side, base_far, side_far))
        here, near = add_parts([(pair, low)] * 2, base, side)
        near = lax.ppermute(near, "head", [(h, h ^ 1) for h in range(peers)])
        dkv = [[here], [near]] + [list(terms) for terms in zip(base_far, side_far)]
    else:
        parts = lax.all_to_all(parts[0], "seq", 0, 0, tiled=True)
        chosen = (jnp.arange(units)[:, None] == wanted[None, :]) & (used[None, :] > 0)
        total = jnp.dot(
            chosen.astype(jnp.bfloat16),
            parts.reshape(parts.shape[0], -1),
            preferred_element_type=jnp.float32,
        )
        dq = exchange_rows(*dq)
        outs = [(kv_heads, jnp.bfloat16)] * peers
        dkv = exchange(add_parts(outs, own, total.reshape(own.shape)))
        dkv = [[piece] for piece in dkv]
    return unpack(me_ref, dq, dkv)


def solution(mesh):
    rows = P(("seq", "head"), None)
    in_specs = (rows, rows, rows, rows, rows, P("seq", "head"), P(None, "head", None))
    return jax.shard_map(
        body, mesh=mesh, in_specs=in_specs, out_specs=(rows, rows, rows), check_vma=False
    )
```
